128 devices in a mesh: by: 16 (over z, x), bx: 8 (over y, core).
Axes of the slice: x: 4, y: 4, z: 4, core: 2. Of those that a mesh axis runs over, the one named last changes fastest.
Arguments:
- features: bfloat16 [512, 128, 256], P(('by', 'bx')), may hold values from -36 to 36
- depth_weight: float32 [512, 64, 128], P(('by', 'bx')), may hold values from 0.05 to 20
- depth_slot: int32 [512, 64, 128], P(('by', 'bx')), may hold values from 0 to 1023
- patch_count: int32 [512], P(('by', 'bx')), may hold values from 1 to 128, 49152 in all
- depth_first: int32 [512], P(('by', 'bx')), may hold values from 0 to 31
- depth_count: int32 [512], P(('by', 'bx')), may hold values from 16 to 32
- tile_dest: int32 [512, 32], P(('by', 'bx')), may hold values from 0 to 127, all different within a row; in each aligned block of 4 rows (0 to 3, 4 to 7, ...) at most 2 rows name the same one
- tile_cells: int32 [512, 1024], P(('by', 'bx')), may hold values from 0 to 1599
- conv_first: bfloat16 [3, 3, 256, 256], replicated, may hold values from -0.125 to 0.125
- conv_second: bfloat16 [3, 3, 256, 256], replicated, may hold values from -0.125 to 0.125
- grad_out: bfloat16 [640, 320, 256], P('by', 'bx'), may hold values from -6 to 6
Outputs:
- out_bev: bfloat16 [640, 320, 256], P('by', 'bx')
- grad_features: bfloat16 [512, 128, 256], P(('by', 'bx'))
- grad_depth_weight: float32 [512, 64, 128], P(('by', 'bx'))
- grad_conv_first: float32 [3, 3, 256, 256], replicated
- grad_conv_second: float32 [3, 3, 256, 256], replicated
The draws below stay inside these ranges and needn't reach their ends.
Inputs may be any that keep to these rules, and one draw needn't show every extreme that they name: `tile_dest`: tile t is the device of index t along by+bx, by the slower; each block names 32 different tiles; the 4 blocks of one device name one tile at most 2 times, a bound that some device reaches. `tile_cells`: cell index inside a tile, row-major over 40 x 40. `depth_slot`: slot s lies in cell list s // 32 of its block. `patch_count`: all blocks together hold 512 * 128 * 3 // 4 live patches; some block is full.
All inputs are finite; a program needn't handle non-finite values.
Results may differ from the reference program's by a relative error of at most 0.0074.
Values may be sent and summed in bfloat16 or wider, within the bound.
No kernel may reach another device: no remote copies, remote signals or barrier semaphores. Data moves between devices by JAX's collectives and lax.ppermute only.
A program may use at most 128 MiB of HBM per device.

```python
import math
import jax
import jax.numpy as jnp
import numpy as np
from jax import lax

C = 256
DB = 64
PB = 128
NB = 4
Q = 32
CAP = 2
TR = 40
TC = 40
K = 32
BLOCKS = 512
GH = 640
GW = 320
N_BX = 8
DEVICES = 128


def touch_ends(values, key, smallest, largest):
    longest = values.shape.index(max(values.shape))
    spots = []
    for shift in (0, 1):
        where = [jax.random.randint(jax.random.fold_in(key, axis), (), 0, length) for axis, length in enumerate(values.shape)]
        where[longest] = (where[longest] + shift) % values.shape[longest]
        spots.append(tuple(where))
    return values.at[spots[0]].set(smallest).at[spots[1]].set(largest)


def shard_levels(rng, extent, shards, low, high):
    def one(axis_at, parts):
        steps = jax.random.uniform(jax.random.fold_in(jax.random.fold_in(rng, 6), axis_at), (parts,), jnp.float32, low / len(shards), high / len(shards))
        return jnp.repeat(jnp.exp(steps), extent[axis_at] // parts).reshape((-1,) + (1,) * (len(extent) - axis_at - 1))

    factor_of = one(*shards[0])
    for cut in shards[1:]:
        factor_of = factor_of * one(*cut)
    return factor_of


def profile(count, total, reach, skew):
    weights = [(1 << 20) // math.isqrt(rank ** skew) + 1 for rank in range(2, count + 1)]
    surplus, counts = total - reach - (count - 1), [1] * (count - 1)
    while surplus > 0:
        candidates = [i for i in range(count - 1) if counts[i] < reach]
        whole, left = sum([weights[i] for i in candidates]), surplus
        for i in candidates:
            extra = min(reach - counts[i], max(1, left * weights[i] // whole), surplus)
            counts[i] = counts[i] + extra
            surplus = surplus - extra
    return np.array([reach] + counts)


def uneven(stream_key, count, total, bound, skew):
    if count == 2:
        one = jax.random.randint(stream_key, (), max(1, total - bound), min(bound, total - 1) + 1)
        return jnp.stack([one, total - one])
    lengths = jnp.asarray(profile(count, total, bound, skew), jnp.int32)
    twos = (count - 1) // 2
    source_of, sink = lengths[1:1 + 2 * twos:2], lengths[2:2 + 2 * twos:2]
    margin = jnp.minimum(source_of - 1, bound - sink)
    passed = jax.random.randint(jax.random.fold_in(stream_key, 1), (twos,), 0, 1 << 20) % (margin + 1)
    lengths = lengths.at[1:1 + 2 * twos:2].set(source_of - passed).at[2:2 + 2 * twos:2].set(sink + passed)
    return lengths[jax.random.permutation(jax.random.fold_in(stream_key, 2), count)]


def routed_block(key, own, number, rows, count, top, limit, lean):
    ranking = jax.random.permutation(key, count)
    heavy_load, ordinary = shares(count, rows * top, limit, lean, True), shares(count, rows * top, limit, lean, False)
    places = jnp.arange(count)

    def named(tallies, offset_by):
        used = int((tallies > 0).sum())
        fixed = max(1, used // 4)
        moved = fixed + (places - fixed + offset_by * (used - fixed)) % max(1, count - fixed)
        return jnp.zeros((count,), jnp.int32).at[ranking[jnp.where(places < fixed, places, moved)]].set(jnp.asarray(tallies, jnp.int32))

    tallies = jnp.where(number % 4 == 0, named(heavy_load, number // 4), named(ordinary, number - number // 4 - 1))
    mixed = jax.random.permutation(jax.random.fold_in(own, 3), count)
    giver, sink = mixed[0:count // 2 * 2:2], mixed[1:count // 2 * 2:2]
    room = jnp.minimum(tallies[giver] - 1, limit - tallies[sink]) // 2
    room = jnp.where((giver == ranking[0]) | (sink == ranking[0]) | (tallies[sink] == 0), 0, jnp.maximum(room, 0))
    moved = jax.random.randint(jax.random.fold_in(own, 4), (count // 2,), 0, 1 << 20) % (room + 1)
    tallies = tallies.at[giver].add(-moved).at[sink].add(moved)
    items = jnp.searchsorted(jnp.cumsum(tallies), jnp.arange(rows * top), side="right").astype(jnp.int32)
    grid = items.reshape(top, rows).T
    grid = grid[jax.random.permutation(jax.random.fold_in(own, 1), rows)]
    offset_by = jax.random.randint(jax.random.fold_in(own, 2), (rows, 1), 0, top)
    return jnp.take_along_axis(grid, (jnp.arange(top)[None, :] + offset_by) % top, axis=1)


def shares(count, total, most, lean, full):
    portions = [(1 << 20) // math.isqrt(standing ** lean) + 1 for standing in range(1, count + 1)]
    largest = most if full else min(most, max(-(-total // count), total * portions[0] // sum(portions)))
    least = 1 if total - largest >= count - 1 else 0
    counts, rest = [largest] + [least] * (count - 1), total - largest - least * (count - 1)
    while rest > 0:
        movable = [i for i in range(1, count) if counts[i] < largest] or [i for i in range(1, count) if counts[i] < most]
        pool, budget = sum([portions[i] for i in movable]), rest
        for i in movable:
            extra = min(most - counts[i], max(1, budget * portions[i] // pool), rest)
            counts[i] = counts[i] + extra
            rest = rest - extra
    return np.array(counts)


def scatter_about(own_key, extent, scale, bound, split=(), kind=jnp.bfloat16):
    level = shard_levels(own_key, extent, split, -0.22, 0.18) if split else 1.0
    values = jax.random.normal(own_key, extent, jnp.float32) * scale * level
    return jnp.minimum(jnp.maximum(values, -bound), bound).astype(kind)


def setup_inputs(seed: int = 0) -> dict:
    streams_of = jax.random.split(jax.random.key(seed), 12)
    features = scatter_about(streams_of[0], (BLOCKS, PB, C), 6.0, 36.0, ((0, 128),))
    depth_weight = jnp.clip(jnp.exp(math.log(20.0) - 5.9914645 * jax.random.uniform(streams_of[1], (BLOCKS, DB, PB), jnp.float32) ** shard_levels(streams_of[1], (BLOCKS, DB, PB), ((0, 128),), -0.2, 0.2)), 0.05, 20.0)
    depth_slot = touch_ends(jax.random.randint(streams_of[2], (BLOCKS, DB, PB), 0, K * Q), jax.random.fold_in(streams_of[2], 1), 0, (K * Q) - 1).astype(jnp.int32)
    patch_count = uneven(streams_of[3], BLOCKS, BLOCKS * PB * 3 // 4, PB, 2).astype(jnp.int32)
    depth_first = touch_ends(jax.random.randint(streams_of[4], (BLOCKS,), 0, DB // 2), jax.random.fold_in(streams_of[4], 1), 0, (DB // 2) - 1).astype(jnp.int32)
    depth_count = touch_ends(jax.random.randint(streams_of[5], (BLOCKS,), DB // 4, DB // 2 + 1), jax.random.fold_in(streams_of[5], 1), DB // 4, (DB // 2 + 1) - 1).astype(jnp.int32)
    tile_dest_keys = jax.random.split(jax.random.fold_in(streams_of[6], 1), BLOCKS // NB)
    tile_dest_turns = jax.random.permutation(jax.random.fold_in(streams_of[6], 3), BLOCKS // NB)
    tile_dest = jax.vmap(lambda own, number: routed_block(jax.random.fold_in(streams_of[6], 2), own, number, NB, DEVICES, K, CAP, 2))(tile_dest_keys, tile_dest_turns).reshape((BLOCKS, K))
    tile_cells = touch_ends(jax.random.randint(streams_of[7], (BLOCKS, K * Q), 0, TR * TC), jax.random.fold_in(streams_of[7], 1), 0, (TR * TC) - 1).astype(jnp.int32)
    conv_first = scatter_about(streams_of[8], (3, 3, C, C), (9 * C) ** -0.5, 0.125)
    conv_second = scatter_about(streams_of[9], (3, 3, C, C), (9 * C) ** -0.5, 0.125)
    grad_out = scatter_about(streams_of[10], (GH, GW, C), 1.0, 6.0, ((0, 16), (1, 8)))
    return dict(features=features, depth_weight=depth_weight, depth_slot=depth_slot, patch_count=patch_count, depth_first=depth_first, depth_count=depth_count, tile_dest=tile_dest, tile_cells=tile_cells, conv_first=conv_first, conv_second=conv_second, grad_out=grad_out)


def lift_block(feature, weights, slot_map, live_count, first_bin, bin_count, slot_space):
    bin_index = jnp.arange(weights.shape[0], dtype=jnp.int32)[:, None]
    range_mask = ((bin_index >= first_bin) & (bin_index < first_bin + bin_count)).astype(weights.dtype)
    live_weight = range_mask * weights
    depth_total = lax.optimization_barrier(jnp.sum(live_weight, axis=0))
    depth_prob = live_weight / depth_total
    patch_index = jnp.arange(feature.shape[0], dtype=jnp.int32)
    patch_mask = (patch_index < live_count).astype(feature.dtype)[:, None]
    masked = feature * patch_mask
    slot_cols = jnp.broadcast_to(patch_index[None, :], slot_map.shape)
    depth_table = jnp.zeros((slot_space, feature.shape[0]), depth_prob.dtype).at[slot_map, slot_cols].add(depth_prob)
    return (depth_table.astype(jnp.bfloat16), masked, depth_prob, depth_total, range_mask, patch_mask)

def conv_same(padded, kernel, tile_rows, tile_cols):
    result = jnp.zeros((tile_rows * tile_cols, kernel.shape[3]), jnp.float32)
    for row_off in range(3):
        for col_off in range(3):
            window = padded[row_off:row_off + tile_rows, col_off:col_off + tile_cols].reshape(tile_rows * tile_cols, -1)
            result = result + jnp.dot(window, kernel[row_off, col_off], preferred_element_type=jnp.float32)
    return result.reshape(tile_rows, tile_cols, -1)

def kernel_grad(padded, cotangent, tile_rows, tile_cols):
    flat_cot = cotangent.reshape(tile_rows * tile_cols, -1)
    tap_rows = []
    for row_off in range(3):
        tap_row = []
        for col_off in range(3):
            window = padded[row_off:row_off + tile_rows, col_off:col_off + tile_cols].reshape(tile_rows * tile_cols, -1)
            tap_row.append(jnp.dot(window.T, flat_cot, preferred_element_type=jnp.float32))
        tap_rows.append(jnp.stack(tap_row))
    return jnp.stack(tap_rows)

def flip_kernel(kernel):
    return jnp.transpose(kernel[::-1, ::-1], (0, 1, 3, 2))

def pad_grid(values):
    return jnp.pad(values, ((1, 1), (1, 1), (0, 0)))

def silu_slope(values):
    sig = jax.nn.sigmoid(values)
    return sig * (1.0 + values * (1.0 - sig))

def global_rows(dest, cells):
    tile_ids = jnp.repeat(dest, Q)
    grid_row = tile_ids // N_BX * TR + cells // TC
    grid_col = tile_ids % N_BX * TC + cells % TC
    return (grid_row * GW + grid_col).astype(jnp.int32)

def reference(features, depth_weight, depth_slot, patch_count, depth_first, depth_count, tile_dest, tile_cells, conv_first, conv_second, grad_out):
    slot_space = tile_cells.shape[1]
    channels = features.shape[2]
    block_data = (features, depth_weight, depth_slot, patch_count, depth_first, depth_count, tile_dest, tile_cells)

    def splat_step(bev_grid, one_block):
        feature, weights, slot_map, live_count, first_bin, bin_count, dest, cells = one_block
        depth_table, masked, depth_prob, depth_total, range_mask, patch_mask = lift_block(feature, weights, slot_map, live_count, first_bin, bin_count, slot_space)
        block_part = jnp.dot(depth_table, masked, preferred_element_type=jnp.float32).astype(jnp.bfloat16)
        flat_index = global_rows(dest, cells)
        return (bev_grid.at[flat_index].add(block_part.astype(bev_grid.dtype)), None)
    start_grid = jnp.zeros((GH * GW, channels), jnp.float32)
    bev_grid, unused = lax.scan(splat_step, start_grid, block_data)
    base = bev_grid.reshape(GH, GW, channels).astype(jnp.bfloat16)
    base_pad = pad_grid(base)
    first_act = conv_same(base_pad, conv_first, GH, GW)
    hidden = jax.nn.silu(first_act).astype(jnp.bfloat16)
    hidden_pad = pad_grid(hidden)
    out_bev = conv_same(hidden_pad, conv_second, GH, GW).astype(jnp.bfloat16)
    grad_second = kernel_grad(hidden_pad, grad_out, GH, GW)
    hidden_cot = conv_same(pad_grid(grad_out), flip_kernel(conv_second), GH, GW)
    first_cot = (hidden_cot * silu_slope(first_act)).astype(jnp.bfloat16)
    grad_first = kernel_grad(base_pad, first_cot, GH, GW)
    base_cot = conv_same(pad_grid(first_cot), flip_kernel(conv_first), GH, GW).astype(jnp.bfloat16).reshape(GH * GW, channels)

    def return_step(one_block):
        feature, weights, slot_map, live_count, first_bin, bin_count, dest, cells = one_block
        depth_table, masked, depth_prob, depth_total, range_mask, patch_mask = lift_block(feature, weights, slot_map, live_count, first_bin, bin_count, slot_space)
        part_cot = jnp.take(base_cot, global_rows(dest, cells), axis=0)
        table_cot = jnp.dot(part_cot, masked.T, preferred_element_type=jnp.float32)
        feature_grad = (jnp.dot(depth_table.T, part_cot, preferred_element_type=jnp.float32) * patch_mask).astype(jnp.bfloat16)
        prob_cot = jnp.take_along_axis(table_cot, slot_map, axis=0)
        weight_grad = range_mask * (prob_cot - lax.optimization_barrier(jnp.sum(depth_prob * prob_cot, axis=0, keepdims=True))) / depth_total
        return (feature_grad, weight_grad)
    grad_features, grad_depth = lax.map(return_step, block_data)
    return (out_bev, grad_features, grad_depth, grad_first, grad_second)
```

```python
from functools import partial

import jax
import jax.numpy as jnp
from jax import lax
from jax.experimental import pallas as pl
from jax.experimental.pallas import tpu as pltpu
from jax.sharding import PartitionSpec as P

CAP = 2
BINS = 64
LIVE = 128
SLOTS = 1024
LIST = 32
LISTS = 32
BLOCKS = 4
CH = 256
TILE = 40
CELLS = TILE * TILE
PITCH = 48
LEAD = 16
FLAT = 2160
WIDE0, WIDE = 48, 2048
CORE0, CORE = 112, 1920
F32 = jnp.float32
BF16 = jnp.bfloat16
VMEM = pl.BlockSpec(memory_space=pltpu.VMEM)
SMEM = pl.BlockSpec(memory_space=pltpu.SMEM)
PARAMS = pltpu.CompilerParams(vmem_limit_bytes=56 * 1024 * 1024)


def call(kernel, ins, out_shape, out_specs, scratch, flops, moved):
    return pl.pallas_call(
        kernel,
        in_specs=ins,
        out_shape=out_shape,
        out_specs=out_specs,
        scratch_shapes=scratch,
        compiler_params=PARAMS,
        cost_estimate=pl.CostEstimate(flops=flops, bytes_accessed=moved, transcendentals=0),
    )


def depth_parts(first_ref, count_ref, weight_ref, b):
    bins = lax.broadcasted_iota(jnp.int32, (BINS, LIVE), 0)
    first = first_ref[b]
    in_range = (bins >= first) & (bins < first + count_ref[b])
    live = jnp.where(in_range, weight_ref[b], 0.0)
    total = jnp.sum(live, axis=0, keepdims=True)
    return in_range, live / total, total


def masked_features(live_ref, feat_ref, b):
    patch = lax.broadcasted_iota(jnp.int32, (LIVE, CH), 0)
    return jnp.where(patch < live_ref[b], feat_ref[b].astype(F32), 0.0).astype(BF16)


def lift_kernel(
    first_ref,
    count_ref,
    live_ref,
    route_ref,
    feat_ref,
    weight_ref,
    slot_ref,
    out_ref,
    table_ref,
    prob,
    part,
):
    def wipe(i, c):
        out_ref[pl.ds(pl.multiple_of(i * 256, 256), 256), :] = jnp.zeros((256, CH), BF16)
        return c

    lax.fori_loop(0, 32, wipe, 0)
    low = lax.broadcasted_iota(jnp.int32, (8, LIVE), 0)

    def block(b, c):
        _, share, _ = depth_parts(first_ref, count_ref, weight_ref, b)
        prob[...] = share
        first = first_ref[b]
        pairs = (count_ref[b] + 1) // 2
        for chunk in range(4):

            def pair(i, acc):
                for step in range(2):
                    d = first + 2 * i + step
                    slot = jnp.broadcast_to(slot_ref[b, pl.ds(d, 1), :], (8, LIVE))
                    share = jnp.broadcast_to(prob[pl.ds(d, 1), :], (8, LIVE))
                    mine = jnp.where((slot & 7) == low, share, 0.0)
                    high = (slot >> 3) - chunk * 32
                    acc = [a + jnp.where(high == r, mine, 0.0) for r, a in enumerate(acc)]
                return acc

            acc = lax.fori_loop(0, pairs, pair, [jnp.zeros((8, LIVE), F32)] * 32)
            table_ref[b, chunk * 256 : (chunk + 1) * 256, :] = jnp.concatenate(acc, axis=0).astype(
                BF16
            )
        part[...] = jnp.dot(
            table_ref[b], masked_features(live_ref, feat_ref, b), preferred_element_type=F32
        ).astype(BF16)
        for k in range(LISTS):
            to = pl.multiple_of(route_ref[b * LISTS + k] * LIST, LIST)
            out_ref[pl.ds(to, LIST), :] = part[k * LIST : (k + 1) * LIST, :]
        return c

    lax.fori_loop(0, BLOCKS, block, 0)


def lift(first, count, live, route, features, weights, slots):
    return call(
        lift_kernel,
        [SMEM] * 4 + [VMEM] * 3,
        (
            jax.ShapeDtypeStruct((128 * CAP * LIST, CH), BF16),
            jax.ShapeDtypeStruct((BLOCKS, SLOTS, LIVE), BF16),
        ),
        (VMEM, VMEM),
        [pltpu.VMEM((BINS, LIVE), F32), pltpu.VMEM((SLOTS, CH), BF16)],
        300_000_000,
        6_000_000,
    )(first, count, live, route, features, weights, slots)


def pack_kernel(dest_ref, cell_ref, out_ref, route_ref, seen):
    def clear(i, c):
        seen[i] = 0
        return c

    lax.fori_loop(0, 128, clear, 0, unroll=8)
    out_ref[...] = jnp.full_like(out_ref, -1)
    for i in range(BLOCKS * LISTS):
        b, k = i // LISTS, i % LISTS
        tile = dest_ref[b, k]
        rank = seen[tile]
        seen[tile] = rank + 1
        to = tile * CAP + rank
        route_ref[i] = to
        out_ref[pl.ds(to, 1), :] = cell_ref[b : b + 1, k * LIST : (k + 1) * LIST]


def packed_cells(dest, cells):
    return call(
        pack_kernel,
        [SMEM, VMEM],
        (
            jax.ShapeDtypeStruct((128 * CAP, LIST), jnp.int32),
            jax.ShapeDtypeStruct((BLOCKS * LISTS,), jnp.int32),
        ),
        (VMEM, SMEM),
        [pltpu.SMEM((128,), jnp.int32)],
        1_000_000,
        100_000,
    )(dest, cells)


def splat_kernel(
    cell_ref, list_ref, gout_ref, base_ref, top_ref, bottom_ref, left_ref, right_ref, acc, hit, strip
):
    rows = 128
    span = 1024
    places = lax.broadcasted_iota(jnp.int32, (rows, span), 0).astype(F32).astype(BF16)
    one, zero = jnp.ones((), BF16), jnp.zeros((), BF16)
    for chunk in range(8):
        cells = cell_ref[chunk : chunk + 1, :]
        low = jnp.broadcast_to((cells & 127).astype(F32), (rows, span)).astype(BF16)
        high = jnp.broadcast_to((cells >> 7).astype(F32), (rows, span)).astype(BF16)
        same = jnp.where(low == places, one, zero)
        for m in range(13):
            end = min(rows, CELLS - m * rows)
            hit[m * rows : m * rows + end, :] = jnp.where(
                high == jnp.full((), m, BF16), same, zero
            )[:end, :]
        part = jnp.dot(
            hit[...], list_ref[chunk * span : (chunk + 1) * span, :], preferred_element_type=F32
        )
        if chunk == 0:
            acc[...] = part
        else:
            acc[...] += part
    base_ref[...] = acc[...].astype(BF16)
    top_ref[:80, :] = acc[:80, :].astype(BF16)
    bottom_ref[:80, :] = acc[CELLS - 80 :, :].astype(BF16)
    for y in range(TILE):
        strip[0, 2 * y : 2 * y + 2, :] = acc[TILE * y : TILE * y + 2, :]
        strip[1, 2 * y : 2 * y + 2, :] = acc[TILE * y + 38 : TILE * y + 40, :]
    left_ref[:80, :] = strip[0].astype(BF16)
    right_ref[:80, :] = strip[1].astype(BF16)
    for n, ref in enumerate((top_ref, bottom_ref, left_ref, right_ref)):
        ref[80:, :] = gout_ref[n]


def splat(cells, lists, gout_edges):
    strip = jax.ShapeDtypeStruct((160, CH), BF16)
    return call(
        splat_kernel,
        [VMEM] * 3,
        (jax.ShapeDtypeStruct((CELLS, CH), BF16),) + (strip,) * 4,
        (VMEM,) * 5,
        [pltpu.VMEM((CELLS, CH), F32), pltpu.VMEM((CELLS, 1024), BF16), pltpu.VMEM((2, 80, CH), F32)],
        6_700_000_000,
        6_000_000,
    )(cells, lists, gout_edges)


def corner_kernel(top_ref, bottom_ref, left_ref, right_ref, up_ref, down_ref):
    for strip_ref, out_ref, at in ((top_ref, up_ref, 0), (bottom_ref, down_ref, 76)):
        for n in range(2):
            out_ref[96 * n : 96 * n + 80, :] = strip_ref[80 * n : 80 * n + 80, :]
            left = left_ref[80 * n : 80 * n + 80, :].astype(F32)[at : at + 4, :]
            right = right_ref[80 * n : 80 * n + 80, :].astype(F32)[at : at + 4, :]
            out_ref[96 * n + 80 : 96 * n + 96, :] = jnp.concatenate(
                [left, right, jnp.zeros((8, CH), F32)], axis=0
            ).astype(BF16)


def with_corners(top, bottom, left, right):
    strip = jax.ShapeDtypeStruct((192, CH), BF16)
    return call(
        corner_kernel, [VMEM] * 4, (strip, strip), (VMEM, VMEM), [], 1_000_000, 600_000
    )(top, bottom, left, right)


def shifted(values, axis, step):
    count = lax.axis_size(axis)
    return lax.ppermute(
        values, axis, [(i, i + step) for i in range(count) if 0 <= i + step < count]
    )


def lay_out(flat, center, above_ref, below_ref, left_ref, right_ref, n):
    above = above_ref[96 * n : 96 * n + 96, :].astype(F32)
    below = below_ref[96 * n : 96 * n + 96, :].astype(F32)
    left = left_ref[80 * n : 80 * n + 80, :].astype(F32)
    right = right_ref[80 * n : 80 * n + 80, :].astype(F32)
    flat[...] = jnp.zeros_like(flat)

    def spot(y, x):
        return 8 + (y + 2) * PITCH + LEAD + x

    for y in range(TILE):
        flat[spot(y, 0) : spot(y, 0) + TILE, :] = center[y * TILE : (y + 1) * TILE, :].astype(F32)
        flat[spot(y, -2) : spot(y, 0), :] = left[2 * y : 2 * y + 2, :]
        flat[spot(y, 40) : spot(y, 42), :] = right[2 * y : 2 * y + 2, :]
    for r in range(2):
        for rows, y in ((above, r - 2), (below, 40 + r)):
            flat[spot(y, 0) : spot(y, 40), :] = rows[r * TILE : (r + 1) * TILE, :]
            flat[spot(y, -2) : spot(y, 0), :] = rows[80 + 2 * r : 82 + 2 * r, :]
            flat[spot(y, 40) : spot(y, 42), :] = rows[84 + 2 * r : 86 + 2 * r, :]


def spread(flat, wide):
    step = 144
    for at in range(0, FLAT, step):
        for j in range(3):
            wide[at : at + step, j * CH : (j + 1) * CH] = flat[at + 7 + j : at + 7 + j + step, :].astype(
                BF16
            )


def taps(wide, weights, start, rows):
    total = None
    for i in range(3):
        at = pl.multiple_of(start + (i - 1) * PITCH, 16)
        part = jnp.dot(
            wide[pl.ds(at, rows), :],
            weights[i * 3 * CH : (i + 1) * 3 * CH, :],
            preferred_element_type=F32,
        )
        total = part if total is None else total + part
    return total


def flip_kernel(first_ref, second_ref, one_ref, two_ref):
    for source, out in ((first_ref, one_ref), (second_ref, two_ref)):
        for tap in range(9):
            taken = source[(8 - tap) * CH : (9 - tap) * CH, :].astype(F32)
            out[tap * CH : (tap + 1) * CH, :] = taken.T.astype(BF16)


def flipped(first, second):
    out = jax.ShapeDtypeStruct((9 * CH, CH), BF16)
    return call(
        flip_kernel, [VMEM] * 2, (out, out), (VMEM, VMEM), [], 10_000_000, 5_000_000
    )(first, second)


def place_mask(by, bx, start, rows, rim):
    n = lax.broadcasted_iota(jnp.int32, (rows, 128), 0) + (start - LEAD + 1)
    line = (n * 87382) >> 22
    x = n - line * PITCH - 1
    y = line - 2
    near = (y >= -rim) & (y < TILE + rim) & (x >= -rim) & (x < TILE + rim)
    gy, gx = y + by * TILE, x + bx * TILE
    inside = near & (gy >= 0) & (gy < 16 * TILE) & (gx >= 0) & (gx < 8 * TILE)
    return jnp.concatenate([jnp.where(inside, 1.0, 0.0)] * 2, axis=1) > 0.5


def kernel_sums(wide, turned, out):
    for tap in range(9):
        i, j = tap // 3, tap % 3
        at = WIDE0 + (i - 1) * PITCH
        got = jnp.dot(
            turned[...], wide[at : at + WIDE, j * CH : (j + 1) * CH], preferred_element_type=F32
        ).T.astype(BF16)
        for h in range(2):
            to = (2 * tap + h) * CH
            out[to : to + CH, :] = got[:, h * 128 : (h + 1) * 128]


def turn(spot_ref, wide, turned):
    for k in range(WIDE // 256):
        at = WIDE0 + k * 256
        inside = place_mask(spot_ref[0], spot_ref[1], at, 256, 0)
        values = wide[at : at + 256, CH : 2 * CH].astype(F32)
        turned[:, k * 256 : (k + 1) * 256] = jnp.where(inside, values, 0.0).T.astype(BF16)


def act_kernel(
    spot_ref,
    first_ref,
    second_ref,
    base_ref,
    gout_ref,
    above_ref,
    below_ref,
    left_ref,
    right_ref,
    hidden_ref,
    fcot_ref,
    sums_ref,
    wide,
    gwide,
    flat,
    flat2,
    turned,
):
    rims = (above_ref, below_ref, left_ref, right_ref)
    lay_out(flat, base_ref, *rims, 0)
    spread(flat, wide)
    lay_out(flat2, gout_ref, *rims, 1)
    spread(flat2, gwide)
    flat[...] = jnp.zeros_like(flat)
    flat2[...] = jnp.zeros_like(flat2)

    def activate(k, c):
        at = pl.multiple_of(WIDE0 + k * 512, 16)
        first_act = taps(wide, first_ref, at, 512)
        hidden_cot = taps(gwide, second_ref, at, 512)
        inside = place_mask(spot_ref[0], spot_ref[1], at, 512, 1)
        sig = jax.nn.sigmoid(first_act)
        to = pl.ds(pl.multiple_of(at + 8, 8), 512)
        flat2[to, :] = jnp.where(inside, first_act * sig, 0.0)
        slope = sig * (1.0 + first_act * (1.0 - sig))
        flat[to, :] = jnp.where(inside, hidden_cot * slope, 0.0)
        return c

    lax.fori_loop(0, WIDE // 512, activate, 0)
    spread(flat, fcot_ref)
    turn(spot_ref, fcot_ref, turned)
    kernel_sums(wide, turned, sums_ref.at[0])
    spread(flat2, hidden_ref)
    turn(spot_ref, gwide, turned)
    kernel_sums(hidden_ref, turned, sums_ref.at[1])


def activate_tile(spot, first, second, base, gout, rims):
    wide = jax.ShapeDtypeStruct((FLAT, 3 * CH), BF16)
    return call(
        act_kernel,
        [SMEM] + [VMEM] * 8,
        (wide, wide, jax.ShapeDtypeStruct((2, 18 * CH, 128), BF16)),
        (VMEM,) * 3,
        [
            pltpu.VMEM((FLAT, 3 * CH), BF16),
            pltpu.VMEM((FLAT, 3 * CH), BF16),
            pltpu.VMEM((FLAT + 16, CH), F32),
            pltpu.VMEM((FLAT + 16, CH), F32),
            pltpu.VMEM((CH, WIDE), BF16),
        ],
        9_000_000_000,
        16_000_000,
    )(spot, first, second, base, gout, *rims)


def strip_pads(got, out, k):
    for r in range(5):
        lines = [got[(2 * r + s) * PITCH : (2 * r + s) * PITCH + TILE, :] for s in range(2)]
        to = pl.multiple_of(k * 400 + r * 80, 16)
        out[pl.ds(to, 80), :] = jnp.concatenate(lines, axis=0).astype(BF16)


def back_kernel(first_ref, cell_ref, fcot_ref, out_ref, tile):
    def back(k, c):
        at = pl.multiple_of(CORE0 + k * 480, 16)
        strip_pads(taps(fcot_ref, first_ref, at, 480), tile, k)
        return c

    lax.fori_loop(0, 4, back, 0)
    tile[CELLS:, :] = jnp.zeros((1664 - CELLS, CH), BF16)
    places = lax.broadcasted_iota(jnp.int32, (512, 128), 1).astype(F32).astype(BF16)
    one, zero = jnp.ones((), BF16), jnp.zeros((), BF16)

    def pick(k, c):
        at = pl.multiple_of(k * 512, 512)
        cells = jnp.broadcast_to(cell_ref[pl.ds(at, 512), :], (512, 128))
        high = (cells >> 7).astype(F32).astype(BF16)
        same = jnp.where((cells & 127).astype(F32).astype(BF16) == places, one, zero)
        hits = [jnp.where(high == jnp.full((), m, BF16), same, zero) for m in range(13)]
        out_ref[pl.ds(at, 512), :] = jnp.dot(
            jnp.concatenate(hits, axis=1), tile[...], preferred_element_type=F32
        ).astype(BF16)
        return c

    lax.fori_loop(0, 16, pick, 0)


def send_back(first, cells, fcot_wide):
    return call(
        back_kernel,
        [VMEM] * 3,
        jax.ShapeDtypeStruct((128 * CAP * LIST, CH), BF16),
        VMEM,
        [pltpu.VMEM((1664, CH), BF16)],
        9_000_000_000,
        12_000_000,
    )(first, cells, fcot_wide)


def out_kernel(second_ref, hidden_ref, out_ref):
    def forward(k, c):
        at = pl.multiple_of(CORE0 + k * 480, 16)
        strip_pads(taps(hidden_ref, second_ref, at, 480), out_ref, k)
        return c

    lax.fori_loop(0, 4, forward, 0)


def outward(second, hidden_wide):
    return call(
        out_kernel,
        [VMEM] * 2,
        jax.ShapeDtypeStruct((CELLS, CH), BF16),
        VMEM,
        [],
        2_300_000_000,
        5_000_000,
    )(second, hidden_wide)


def widen_kernel(sums_ref, one_ref, two_ref):
    for by in range(16):
        for bx in range(8):
            values = sums_ref[bx, by].astype(F32)
            at = (by * 8 + bx) * 72
            done = 0
            while done < 72:
                part, row = divmod(at + done, CH)
                n, part = divmod(part, 18)
                size = min(72 - done, CH - row)
                out = (one_ref, two_ref)[n]
                lanes = slice(part % 2 * 128, part % 2 * 128 + 128)
                out[part // 2, row : row + size, lanes] = values[done : done + size, :]
                done += size


def widen(sums):
    out = jax.ShapeDtypeStruct((9, CH, CH), F32)
    return call(widen_kernel, [VMEM], (out, out), (VMEM, VMEM), [], 1_000_000, 7_000_000)(sums)


def settle_kernel(first_ref, count_ref, live_ref, route_ref, feat_ref, weight_ref, slot_ref, table_ref, back_ref, gfeat_ref, gweight_ref, part, cot, pick):
    for b in range(BLOCKS):
        for k in range(LISTS):
            at = pl.multiple_of(route_ref[b * LISTS + k] * LIST, LIST)
            part[k * LIST : (k + 1) * LIST, :] = back_ref[pl.ds(at, LIST), :]
        masked = masked_features(live_ref, feat_ref, b)
        cot[...] = lax.dot_general(
            part[...], masked, (((1,), (1,)), ((), ())), preferred_element_type=F32
        )
        got = jnp.dot(table_ref[b], part[...], preferred_element_type=F32)
        patch = lax.broadcasted_iota(jnp.int32, (LIVE, CH), 0)
        gfeat_ref[b] = jnp.where(patch < live_ref[b], got, 0.0).astype(BF16)
        pick[...] = jnp.zeros_like(pick)
        first = first_ref[b]

        def eight(q, c):
            at = pl.multiple_of(q * 8, 8)
            slot = slot_ref[b, pl.ds(at, 8), :]
            low, high = slot & 7, slot >> 3

            def group(g, acc):
                for r in range(16):
                    row = g * 16 + r
                    rows = cot[pl.ds(pl.multiple_of(row * 8, 8), 8), :]
                    found = jnp.take_along_axis(rows, low, axis=0, mode="promise_in_bounds")
                    acc = jnp.where(high == row, found, acc)
                return acc

            pick[pl.ds(at, 8), :] = lax.fori_loop(0, 8, group, jnp.zeros((8, LIVE), F32))
            return c

        lax.fori_loop(first >> 3, (first + count_ref[b] + 7) >> 3, eight, 0)
        in_range, prob, total = depth_parts(first_ref, count_ref, weight_ref, b)
        picked = pick[...]
        mean = jnp.sum(prob * picked, axis=0, keepdims=True)
        gweight_ref[b] = jnp.where(in_range, (picked - mean) / total, 0.0)


def settle(first, count, live, route, features, weights, slots, table, back):
    return call(
        settle_kernel,
        [SMEM] * 4 + [VMEM] * 5,
        (
            jax.ShapeDtypeStruct((BLOCKS, LIVE, CH), BF16),
            jax.ShapeDtypeStruct((BLOCKS, BINS, LIVE), F32),
        ),
        (VMEM, VMEM),
        [
            pltpu.VMEM((SLOTS, CH), BF16),
            pltpu.VMEM((SLOTS, LIVE), F32),
            pltpu.VMEM((BINS, LIVE), F32),
        ],
        600_000_000,
        8_000_000,
    )(first, count, live, route, features, weights, slots, table, back)


def exchanged(values):
    return lax.all_to_all(values, ("by", "bx"), split_axis=0, concat_axis=0, tiled=True)


def on_device(
    features,
    depth_weight,
    depth_slot,
    patch_count,
    depth_first,
    depth_count,
    tile_dest,
    tile_cells,
    conv_first,
    conv_second,
    grad_out,
):
    by, bx = lax.axis_index("by"), lax.axis_index("bx")
    me = by * lax.axis_size("bx") + bx
    devices = lax.axis_size("by") * lax.axis_size("bx")
    spot = jnp.stack([by, bx]).astype(jnp.int32)
    groups = BLOCKS * LISTS
    first_taps = conv_first.reshape(9 * CH, CH)
    second_taps = conv_second.reshape(9 * CH, CH)

    cells, route = packed_cells(tile_dest, tile_cells)
    cells = exchanged(cells.reshape(devices, CAP, LIST)).reshape(devices * CAP * LIST)
    cell_column = cells.reshape(-1, 1)
    outgoing, table = lift(
        depth_first, depth_count, patch_count, route, features, depth_weight, depth_slot
    )
    arrived = exchanged(outgoing)

    _, edge = lax.optimization_barrier((outgoing, grad_out))
    gout_edges = jnp.stack(
        [
            edge[:2].reshape(80, CH),
            edge[38:].reshape(80, CH),
            edge[:, :2].reshape(80, CH),
            edge[:, 38:].reshape(80, CH),
        ]
    )
    turned_table = jnp.swapaxes(table, 1, 2)
    _, first_late, second_late = lax.optimization_barrier((outgoing, first_taps, second_taps))
    first_flip, second_flip = flipped(first_late, second_late)
    arrived, cell_column, turned_table, first_flip, second_flip = lax.optimization_barrier(
        (arrived, cell_column, turned_table, first_flip, second_flip)
    )

    base, top, bottom, left, right = splat(cells.reshape(8, 1024), arrived, gout_edges)
    from_left, from_right = shifted(right, "bx", 1), shifted(left, "bx", -1)
    up, down = with_corners(top, bottom, from_left, from_right)
    rims = (shifted(down, "by", 1), shifted(up, "by", -1), from_left, from_right)
    hidden_wide, fcot_wide, sums = activate_tile(
        spot, first_taps, second_flip, base, grad_out.reshape(CELLS, CH), rims
    )
    sums = exchanged(sums.reshape(devices, 72, 128))
    returning = send_back(first_flip, cell_column, fcot_wide)
    returning, sums = lax.optimization_barrier((returning, sums))
    sums = jnp.sum(sums.astype(F32), axis=0).astype(BF16)
    sums = lax.all_to_all(
        jnp.broadcast_to(sums, (16, 72, 128)), "by", split_axis=0, concat_axis=0, tiled=True
    )
    returning, sums = lax.optimization_barrier((returning, sums))
    sums = lax.all_gather(sums, "bx", axis=0)
    returned = exchanged(returning)
    out_bev = outward(second_taps, hidden_wide)
    returned, out_bev = lax.optimization_barrier((returned, out_bev))
    feature_grad, weight_grad = settle(
        depth_first,
        depth_count,
        patch_count,
        route,
        features,
        depth_weight,
        depth_slot,
        turned_table,
        returned,
    )
    sums, weight_grad = lax.optimization_barrier((sums, weight_grad))
    grad_first, grad_second = widen(sums)
    return (
        out_bev.reshape(TILE, TILE, CH),
        feature_grad,
        weight_grad,
        grad_first.reshape(3, 3, CH, CH),
        grad_second.reshape(3, 3, CH, CH),
    )


def solution(mesh):
    placed = (
        P(("by", "bx"), None, None),
        P(("by", "bx"), None, None),
        P(("by", "bx"), None, None),
        P(("by", "bx")),
        P(("by", "bx")),
        P(("by", "bx")),
        P(("by", "bx"), None),
        P(("by", "bx"), None),
        P(),
        P(),
        P("by", "bx", None),
    )
    return jax.shard_map(
        on_device,
        mesh=mesh,
        in_specs=placed,
        out_specs=(
            P("by", "bx", None),
            P(("by", "bx"), None, None),
            P(("by", "bx"), None, None),
            P(),
            P(),
        ),
        check_vma=False,
    )
```

```python
from functools import partial

import jax
import jax.numpy as jnp
from jax import lax
from jax.experimental import pallas as pl
from jax.experimental.pallas import tpu as pltpu
from jax.sharding import PartitionSpec as P

CAP = 2
BINS = 64
LIVE = 128
SLOTS = 1024
LIST = 32
LISTS = 32
BLOCKS = 4
CH = 256
TILE = 40
CELLS = TILE * TILE
PITCH = 48
LEAD = 16
FLAT = 2160
WIDE0, WIDE = 48, 2048
CORE0, CORE = 112, 1920
F32 = jnp.float32
BF16 = jnp.bfloat16
VMEM = pl.BlockSpec(memory_space=pltpu.VMEM)
SMEM = pl.BlockSpec(memory_space=pltpu.SMEM)
ANY = pl.BlockSpec(memory_space=pl.ANY)
DMA = pltpu.SemaphoreType.DMA
SENT = 144
SHARE = 72
BACK = 168
PARAMS = pltpu.CompilerParams(vmem_limit_bytes=56 * 1024 * 1024)


def call(kernel, ins, out_shape, out_specs, scratch, flops, moved, **more):
    return pl.pallas_call(
        kernel,
        in_specs=ins,
        out_shape=out_shape,
        out_specs=out_specs,
        scratch_shapes=scratch,
        compiler_params=PARAMS,
        cost_estimate=pl.CostEstimate(flops=flops, bytes_accessed=moved, transcendentals=0),
        **more,
    )


def depth_parts(first_ref, count_ref, weight_ref, b):
    bins = lax.broadcasted_iota(jnp.int32, (BINS, LIVE), 0)
    first = first_ref[b]
    in_range = (bins >= first) & (bins < first + count_ref[b])
    live = jnp.where(in_range, weight_ref[b], 0.0)
    total = jnp.sum(live, axis=0, keepdims=True)
    return in_range, live / total, total


def masked_features(live_ref, feat_ref, b):
    patch = lax.broadcasted_iota(jnp.int32, (LIVE, CH), 0)
    return jnp.where(patch < live_ref[b], feat_ref[b].astype(F32), 0.0).astype(BF16)


def lift_kernel(
    first_ref,
    count_ref,
    live_ref,
    dest_ref,
    feat_ref,
    weight_ref,
    slot_ref,
    cell_ref,
    out_ref,
    table_ref,
    route_ref,
    prob,
    part,
    seen,
    spread_cells,
    code,
):
    def clear(i, c):
        seen[i] = 0
        return c

    lax.fori_loop(0, 128, clear, 0, unroll=8)

    def wipe(i, c):
        out_ref[i] = jnp.zeros((SENT, 128), BF16)
        return c

    lax.fori_loop(0, 128, wipe, 0)
    code[...] = jnp.full_like(code, -1)
    quarter = lax.broadcasted_iota(jnp.int32, (8, 128), 1) >> 5
    for k in range(LISTS):
        cells = cell_ref[:, k // 4 * 128 : k // 4 * 128 + 128]
        one = jnp.where(quarter == k % 4, jnp.concatenate([cells, cells], axis=0), 0)
        two = one + pltpu.roll(one, 32, 1)
        spread_cells[k] = two + pltpu.roll(two, 64, 1)
    half = (lax.broadcasted_iota(jnp.int32, (1, 128), 1) >> 5) & 1
    for i in range(BLOCKS * LISTS):
        b, k = i // LISTS, i % LISTS
        tile = dest_ref[b, k]
        rank = seen[tile]
        seen[tile] = rank + 1
        route_ref[i] = tile * CAP + rank
        code[pl.ds(tile, 1), :] = jnp.where(
            half == rank, spread_cells[k, b : b + 1, :], code[pl.ds(tile, 1), :]
        )
    row = lax.broadcasted_iota(jnp.int32, (16, 128), 0)
    high, low = (code[...] >> 7).astype(F32), (code[...] & 127).astype(F32)
    for d in range(128):
        out_ref[d, 128:SENT, :] = jnp.where(
            row == 0, high[d : d + 1, :], jnp.where(row == 1, low[d : d + 1, :], 0.0)
        ).astype(BF16)
    low = lax.broadcasted_iota(jnp.int32, (8, LIVE), 0)

    def block(b, c):
        _, share, _ = depth_parts(first_ref, count_ref, weight_ref, b)
        prob[...] = share
        first = first_ref[b]
        quads = (count_ref[b] + 3) // 4
        for chunk in range(4):

            def quad(i, acc):
                for step in range(4):
                    d = jnp.minimum(first + 4 * i + step, BINS - 1)
                    slot = jnp.broadcast_to(slot_ref[b, pl.ds(d, 1), :], (8, LIVE))
                    share = jnp.broadcast_to(prob[pl.ds(d, 1), :], (8, LIVE))
                    mine = jnp.where((slot & 7) == low, share, 0.0)
                    high = (slot >> 3) - chunk * 32
                    acc = [a + jnp.where(high == r, mine, 0.0) for r, a in enumerate(acc)]
                return acc

            acc = lax.fori_loop(0, quads, quad, [jnp.zeros((8, LIVE), F32)] * 32)
            table_ref[b, chunk * 256 : (chunk + 1) * 256, :] = jnp.concatenate(acc, axis=0).astype(
                BF16
            )
        part[...] = jnp.dot(
            table_ref[b], masked_features(live_ref, feat_ref, b), preferred_element_type=F32
        ).astype(BF16)
        for k in range(LISTS):
            to = route_ref[b * LISTS + k]
            for h in range(2):
                at = pl.multiple_of((to & 1) * 64 + h * LIST, LIST)
                out_ref[to >> 1, pl.ds(at, LIST), :] = part[
                    k * LIST : (k + 1) * LIST, h * 128 : (h + 1) * 128
                ]
        return c

    lax.fori_loop(0, BLOCKS, block, 0)


def lift(first, count, live, dest, features, weights, slots, cells):
    return call(
        lift_kernel,
        [SMEM] * 4 + [VMEM] * 4,
        (
            jax.ShapeDtypeStruct((128, SENT, 128), BF16),
            jax.ShapeDtypeStruct((BLOCKS, SLOTS, LIVE), BF16),
            jax.ShapeDtypeStruct((BLOCKS * LISTS,), jnp.int32),
        ),
        (VMEM, VMEM, SMEM),
        [
            pltpu.VMEM((BINS, LIVE), F32),
            pltpu.VMEM((SLOTS, CH), BF16),
            pltpu.SMEM((128,), jnp.int32),
            pltpu.VMEM((LISTS, 8, 128), jnp.int32),
            pltpu.VMEM((128, 128), jnp.int32),
        ],
        300_000_000,
        6_000_000,
    )(first, count, live, dest, features, weights, slots, cells)


def splat_kernel(
    list_ref,
    gout_ref,
    base_ref,
    top_ref,
    bottom_ref,
    left_ref,
    right_ref,
    acc,
    hit,
    strip,
    lists,
    code,
):
    rows = 128
    span = 1024
    places = lax.broadcasted_iota(jnp.int32, (rows, span), 0).astype(F32).astype(BF16)
    first_half = lax.broadcasted_iota(jnp.int32, (1, 128), 1) < 64
    one, zero = jnp.ones((), BF16), jnp.zeros((), BF16)
    for n in range(64):
        codes = [list_ref[2 * n + e, 128:SENT, :].astype(F32) for e in range(2)]
        for i in range(2):
            code[n // 8 * 2 + i : n // 8 * 2 + i + 1, n % 8 * 128 : n % 8 * 128 + 128] = jnp.where(
                first_half, codes[0][i : i + 1, :], codes[1][i : i + 1, :]
            )
    for chunk in range(8):
        for n in range(16):
            d = chunk * 16 + n
            for r in range(CAP):
                for h in range(2):
                    at = (n * CAP + r) * LIST
                    lists[at : at + LIST, h * 128 : (h + 1) * 128] = list_ref[
                        d, r * 64 + h * LIST : r * 64 + (h + 1) * LIST, :
                    ]
        high, low = [
            jnp.broadcast_to(code[2 * chunk + i : 2 * chunk + i + 1, :], (rows, span)).astype(BF16)
            for i in range(2)
        ]
        same = jnp.where(low == places, one, zero)
        for m in range(13):
            end = min(rows, CELLS - m * rows)
            hit[m * rows : m * rows + end, :] = jnp.where(
                high == jnp.full((), m, BF16), same, zero
            )[:end, :]
        part = jnp.dot(hit[...], lists[...], preferred_element_type=F32)
        if chunk == 0:
            acc[...] = part
        else:
            acc[...] += part
    base_ref[...] = acc[...].astype(BF16)
    top_ref[:80, :] = acc[:80, :].astype(BF16)
    bottom_ref[:80, :] = acc[CELLS - 80 :, :].astype(BF16)
    for y in range(TILE):
        strip[0, 2 * y : 2 * y + 2, :] = acc[TILE * y : TILE * y + 2, :]
        strip[1, 2 * y : 2 * y + 2, :] = acc[TILE * y + 38 : TILE * y + 40, :]
    left_ref[:80, :] = strip[0].astype(BF16)
    right_ref[:80, :] = strip[1].astype(BF16)
    for n, ref in enumerate((top_ref, bottom_ref, left_ref, right_ref)):
        ref[80:, :] = gout_ref[n]


def splat(lists, gout_edges):
    strip = jax.ShapeDtypeStruct((160, CH), BF16)
    return call(
        splat_kernel,
        [VMEM] * 2,
        (jax.ShapeDtypeStruct((CELLS, CH), BF16),) + (strip,) * 4,
        (VMEM,) * 5,
        [
            pltpu.VMEM((CELLS, CH), F32),
            pltpu.VMEM((CELLS, 1024), BF16),
            pltpu.VMEM((2, 80, CH), F32),
            pltpu.VMEM((1024, CH), BF16),
            pltpu.VMEM((16, 1024), F32),
        ],
        6_700_000_000,
        6_000_000,
    )(lists, gout_edges)


def corner_kernel(top_ref, bottom_ref, left_ref, right_ref, up_ref, down_ref):
    for strip_ref, out_ref, at in ((top_ref, up_ref, 0), (bottom_ref, down_ref, 76)):
        for n in range(2):
            out_ref[96 * n : 96 * n + 80, :] = strip_ref[80 * n : 80 * n + 80, :]
            left = left_ref[80 * n : 80 * n + 80, :].astype(F32)[at : at + 4, :]
            right = right_ref[80 * n : 80 * n + 80, :].astype(F32)[at : at + 4, :]
            out_ref[96 * n + 80 : 96 * n + 96, :] = jnp.concatenate(
                [left, right, jnp.zeros((8, CH), F32)], axis=0
            ).astype(BF16)


def with_corners(top, bottom, left, right):
    strip = jax.ShapeDtypeStruct((192, CH), BF16)
    return call(
        corner_kernel, [VMEM] * 4, (strip, strip), (VMEM, VMEM), [], 1_000_000, 600_000
    )(top, bottom, left, right)


def shifted(values, axis, step):
    count = lax.axis_size(axis)
    return lax.ppermute(
        values, axis, [(i, i + step) for i in range(count) if 0 <= i + step < count]
    )


def lay_out(flat, center, above_ref, below_ref, left_ref, right_ref, n):
    above = above_ref[96 * n : 96 * n + 96, :].astype(F32)
    below = below_ref[96 * n : 96 * n + 96, :].astype(F32)
    left = left_ref[80 * n : 80 * n + 80, :].astype(F32)
    right = right_ref[80 * n : 80 * n + 80, :].astype(F32)
    flat[...] = jnp.zeros_like(flat)

    def spot(y, x):
        return 8 + (y + 2) * PITCH + LEAD + x

    for y in range(TILE):
        flat[spot(y, 0) : spot(y, 0) + TILE, :] = center[y * TILE : (y + 1) * TILE, :].astype(F32)
        flat[spot(y, -2) : spot(y, 0), :] = left[2 * y : 2 * y + 2, :]
        flat[spot(y, 40) : spot(y, 42), :] = right[2 * y : 2 * y + 2, :]
    for r in range(2):
        for rows, y in ((above, r - 2), (below, 40 + r)):
            flat[spot(y, 0) : spot(y, 40), :] = rows[r * TILE : (r + 1) * TILE, :]
            flat[spot(y, -2) : spot(y, 0), :] = rows[80 + 2 * r : 82 + 2 * r, :]
            flat[spot(y, 40) : spot(y, 42), :] = rows[84 + 2 * r : 86 + 2 * r, :]


def spread(flat, wide):
    step = 144
    for at in range(0, FLAT, step):
        for j in range(3):
            wide[at : at + step, j * CH : (j + 1) * CH] = flat[at + 7 + j : at + 7 + j + step, :].astype(
                BF16
            )


def taps(wide, weights, start, rows):
    total = None
    for i in range(3):
        at = pl.multiple_of(start + (i - 1) * PITCH, 16)
        part = jnp.dot(
            wide[pl.ds(at, rows), :],
            weights[i * 3 * CH : (i + 1) * 3 * CH, :],
            preferred_element_type=F32,
        )
        total = part if total is None else total + part
    return total


def flip_kernel(first_ref, second_ref, one_ref, two_ref):
    for source, out in ((first_ref, one_ref), (second_ref, two_ref)):
        for tap in range(9):
            taken = source[(8 - tap) * CH : (9 - tap) * CH, :].astype(F32)
            out[tap * CH : (tap + 1) * CH, :] = taken.T.astype(BF16)


def flipped(first, second):
    out = jax.ShapeDtypeStruct((9 * CH, CH), BF16)
    return call(
        flip_kernel, [VMEM] * 2, (out, out), (VMEM, VMEM), [], 10_000_000, 5_000_000
    )(first, second)


def place_mask(by, bx, start, rows, rim):
    n = lax.broadcasted_iota(jnp.int32, (rows, 128), 0) + (start - LEAD + 1)
    line = (n * 87382) >> 22
    x = n - line * PITCH - 1
    y = line - 2
    near = (y >= -rim) & (y < TILE + rim) & (x >= -rim) & (x < TILE + rim)
    gy, gx = y + by * TILE, x + bx * TILE
    inside = near & (gy >= 0) & (gy < 16 * TILE) & (gx >= 0) & (gx < 8 * TILE)
    return jnp.concatenate([jnp.where(inside, 1.0, 0.0)] * 2, axis=1) > 0.5


def kernel_sums(wide, turned, out):
    for tap in range(9):
        i, j = tap // 3, tap % 3
        at = WIDE0 + (i - 1) * PITCH
        got = jnp.dot(
            turned[...], wide[at : at + WIDE, j * CH : (j + 1) * CH], preferred_element_type=F32
        ).T.astype(BF16)
        for h in range(2):
            to = (2 * tap + h) * CH
            out[to : to + CH, :] = got[:, h * 128 : (h + 1) * 128]


def turn(spot_ref, rows_at, turned):
    for k in range(WIDE // 256):
        at = WIDE0 + k * 256
        inside = place_mask(spot_ref[0], spot_ref[1], at, 256, 0)
        turned[:, k * 256 : (k + 1) * 256] = jnp.where(inside, rows_at(at), 0.0).T.astype(BF16)


def act_kernel(
    spot_ref,
    first_hbm,
    second_hbm,
    base_ref,
    gout_ref,
    above_ref,
    below_ref,
    left_ref,
    right_ref,
    hidden_ref,
    fcot_ref,
    sums_ref,
    first_ref,
    second_ref,
    wide,
    gwide,
    flat,
    flat2,
    turned,
    arrive,
):
    loads = (
        pltpu.make_async_copy(first_hbm, first_ref, arrive.at[0]),
        pltpu.make_async_copy(second_hbm, second_ref, arrive.at[1]),
    )
    for load in loads:
        load.start()
    rims = (above_ref, below_ref, left_ref, right_ref)
    lay_out(flat, base_ref, *rims, 0)
    spread(flat, wide)
    lay_out(flat2, gout_ref, *rims, 1)
    spread(flat2, gwide)
    flat[...] = jnp.zeros_like(flat)
    flat2[...] = jnp.zeros_like(flat2)
    for load in loads:
        load.wait()

    def activate(k, c):
        at = pl.multiple_of(WIDE0 + k * 512, 16)
        first_act = taps(wide, first_ref, at, 512)
        hidden_cot = taps(gwide, second_ref, at, 512)
        inside = place_mask(spot_ref[0], spot_ref[1], at, 512, 1)
        sig = jax.nn.sigmoid(first_act)
        to = pl.ds(pl.multiple_of(at + 8, 8), 512)
        flat2[to, :] = jnp.where(inside, first_act * sig, 0.0)
        slope = sig * (1.0 + first_act * (1.0 - sig))
        flat[to, :] = jnp.where(inside, hidden_cot * slope, 0.0)
        return c

    lax.fori_loop(0, WIDE // 512, activate, 0)
    fcot_ref[...] = flat[8 : 8 + FLAT, :].astype(BF16)
    hidden_ref[...] = flat2[8 : 8 + FLAT, :].astype(BF16)
    turn(spot_ref, lambda at: flat[at + 8 : at + 264, :], turned)
    kernel_sums(wide, turned, sums_ref.at[0])
    spread(flat2, wide)
    turn(spot_ref, lambda at: gwide[at : at + 256, CH : 2 * CH].astype(F32), turned)
    kernel_sums(wide, turned, sums_ref.at[1])


def activate_tile(spot, first, second, base, gout, rims):
    flat = jax.ShapeDtypeStruct((FLAT, CH), BF16)
    return call(
        act_kernel,
        [SMEM, ANY, ANY] + [VMEM] * 6,
        (flat, flat, jax.ShapeDtypeStruct((2, 18 * CH, 128), BF16)),
        (VMEM,) * 3,
        [
            pltpu.VMEM((9 * CH, CH), BF16),
            pltpu.VMEM((9 * CH, CH), BF16),
            pltpu.VMEM((FLAT, 3 * CH), BF16),
            pltpu.VMEM((FLAT, 3 * CH), BF16),
            pltpu.VMEM((FLAT + 16, CH), F32),
            pltpu.VMEM((FLAT + 16, CH), F32),
            pltpu.VMEM((CH, WIDE), BF16),
            DMA((2,)),
        ],
        9_000_000_000,
        9_000_000,
    )(spot, first, second, base, gout, *rims)


def respread(values_ref, flat, wide):
    flat[...] = jnp.zeros_like(flat)
    flat[8 : 8 + FLAT, :] = values_ref[...].astype(F32)
    spread(flat, wide)


def strip_pads(got, out, k):
    for r in range(5):
        lines = [got[(2 * r + s) * PITCH : (2 * r + s) * PITCH + TILE, :] for s in range(2)]
        to = pl.multiple_of(k * 400 + r * 80, 16)
        out[pl.ds(to, 80), :] = jnp.concatenate(lines, axis=0).astype(BF16)


def back_kernel(first_ref, cell_ref, fcot_ref, out_ref, tile, flat, wide):
    respread(fcot_ref, flat, wide)

    def back(k, c):
        at = pl.multiple_of(CORE0 + k * 480, 16)
        strip_pads(taps(wide, first_ref, at, 480), tile, k)
        return c

    lax.fori_loop(0, 4, back, 0)
    tile[CELLS:, :] = jnp.zeros((1664 - CELLS, CH), BF16)
    places = lax.broadcasted_iota(jnp.int32, (512, 128), 1).astype(F32).astype(BF16)
    one, zero = jnp.ones((), BF16), jnp.zeros((), BF16)

    def pick(k, c):
        at = pl.multiple_of(k * 512, 512)
        cells = jnp.broadcast_to(cell_ref[pl.ds(at, 512), :], (512, 128))
        high = (cells >> 7).astype(F32).astype(BF16)
        same = jnp.where((cells & 127).astype(F32).astype(BF16) == places, one, zero)
        hits = [jnp.where(high == jnp.full((), m, BF16), same, zero) for m in range(13)]
        got = jnp.dot(
            jnp.concatenate(hits, axis=1), tile[...], preferred_element_type=F32
        ).astype(BF16)
        for n in range(16):
            for h in range(2):
                at = (n % 2) * 64 + h * LIST
                out_ref[k * 8 + n // 2, at : at + LIST, :] = got[
                    n * LIST : (n + 1) * LIST, h * 128 : (h + 1) * 128
                ]
        return c

    lax.fori_loop(0, 16, pick, 0)


def send_back(first, cells, fcot):
    return call(
        back_kernel,
        [VMEM] * 3,
        jax.ShapeDtypeStruct((128, BACK, 128), BF16),
        VMEM,
        [
            pltpu.VMEM((1664, CH), BF16),
            pltpu.VMEM((FLAT + 16, CH), F32),
            pltpu.VMEM((FLAT, 3 * CH), BF16),
        ],
        9_000_000_000,
        12_000_000,
    )(first, cells, fcot)


def add_share(parts, back):
    total = jnp.sum(parts.astype(F32), axis=0)
    halves = jnp.stack([total[:40], total[32:]]).astype(BF16)
    beside = jnp.broadcast_to(halves, (64, 2, 40, 128)).reshape(128, 40, 128)
    return lax.dynamic_update_slice(back, beside, (0, 128, 0))


def out_kernel(second_ref, hidden_ref, out_ref, flat, wide):
    respread(hidden_ref, flat, wide)

    def forward(k, c):
        at = pl.multiple_of(CORE0 + k * 480, 16)
        strip_pads(taps(wide, second_ref, at, 480), out_ref, k)
        return c

    lax.fori_loop(0, 4, forward, 0)


def outward(second, hidden_wide):
    return call(
        out_kernel,
        [VMEM] * 2,
        jax.ShapeDtypeStruct((CELLS, CH), BF16),
        VMEM,
        [pltpu.VMEM((FLAT + 16, CH), F32), pltpu.VMEM((FLAT, 3 * CH), BF16)],
        2_300_000_000,
        5_000_000,
    )(second, hidden_wide)


def widen_kernel(spot_ref, own_ref, other_ref, one_hbm, two_hbm, one, two, sent):
    odd = spot_ref[1] % 2 == 1
    copies = [
        pltpu.make_async_copy(wide.at[tap], hbm.at[tap], sent.at[9 * n + tap])
        for n, (wide, hbm) in enumerate(((one, one_hbm), (two, two_hbm)))
        for tap in range(9)
    ]
    for device in range(128):
        own, other = own_ref[device].astype(F32), other_ref[device].astype(F32)
        low, high = jnp.where(odd, other, own), jnp.where(odd, own, other)
        values = jnp.concatenate([low, high[8:, :]], axis=0)
        done = 0
        while done < SHARE:
            part, row = divmod(device * SHARE + done, CH)
            n, part = divmod(part, 18)
            size = min(SHARE - done, CH - row)
            lanes = slice(part % 2 * 128, part % 2 * 128 + 128)
            (one, two)[n][part // 2, row : row + size, lanes] = values[done : done + size, :]
            done += size
            if row + size == CH and part % 2 == 1:
                copies[9 * n + part // 2].start()
    for copy in copies:
        copy.wait()


def widen(spot, own, other):
    out = jax.ShapeDtypeStruct((9, CH, CH), F32)
    wide = pltpu.VMEM((9, CH, CH), F32)
    return call(
        widen_kernel,
        [SMEM, VMEM, VMEM],
        (out, out),
        (ANY, ANY),
        [wide, wide, DMA((18,))],
        1_000_000,
        7_000_000,
    )(spot, own, other)


def settle_kernel(
    first_ref,
    count_ref,
    live_ref,
    route_ref,
    feat_ref,
    weight_ref,
    slot_ref,
    table_ref,
    back_ref,
    gfeat_ref,
    gweight_ref,
    part,
    cot,
    pick,
):
    for b in range(BLOCKS):
        for k in range(LISTS):
            to = route_ref[b * LISTS + k]
            rows = pl.ds(pl.multiple_of((to & 1) * 64, 64), 64)
            part[b * LISTS + k] = back_ref[to >> 1, rows, :]
        got = part[b * LISTS : (b + 1) * LISTS]
        lists = jnp.concatenate(
            [got[:, h * LIST : (h + 1) * LIST, :].reshape(SLOTS, 128) for h in range(2)], axis=1
        )
        masked = masked_features(live_ref, feat_ref, b)
        cot[...] = lax.dot_general(
            lists, masked, (((1,), (1,)), ((), ())), preferred_element_type=F32
        )
        got = jnp.dot(table_ref[b], lists, preferred_element_type=F32)
        patch = lax.broadcasted_iota(jnp.int32, (LIVE, CH), 0)
        gfeat_ref[b] = jnp.where(patch < live_ref[b], got, 0.0).astype(BF16)
        pick[...] = jnp.zeros_like(pick)
        first = first_ref[b]

        def eight(q, c):
            at = pl.multiple_of(q * 8, 8)
            slot = slot_ref[b, pl.ds(at, 8), :]
            low, high = slot & 7, slot >> 3

            def group(g, acc):
                for r in range(16):
                    row = g * 16 + r
                    rows = cot[pl.ds(pl.multiple_of(row * 8, 8), 8), :]
                    found = jnp.take_along_axis(rows, low, axis=0, mode="promise_in_bounds")
                    acc = jnp.where(high == row, found, acc)
                return acc

            pick[pl.ds(at, 8), :] = lax.fori_loop(0, 8, group, jnp.zeros((8, LIVE), F32))
            return c

        lax.fori_loop(first >> 3, (first + count_ref[b] + 7) >> 3, eight, 0)
        in_range, prob, total = depth_parts(first_ref, count_ref, weight_ref, b)
        picked = pick[...]
        mean = jnp.sum(prob * picked, axis=0, keepdims=True)
        gweight_ref[b] = jnp.where(in_range, (picked - mean) / total, 0.0)


def settle(first, count, live, route, features, weights, slots, table, back):
    return call(
        settle_kernel,
        [SMEM] * 4 + [VMEM] * 5,
        (
            jax.ShapeDtypeStruct((BLOCKS, LIVE, CH), BF16),
            jax.ShapeDtypeStruct((BLOCKS, BINS, LIVE), F32),
        ),
        (VMEM, VMEM),
        [
            pltpu.VMEM((BLOCKS * LISTS, CAP * LIST, 128), BF16),
            pltpu.VMEM((SLOTS, LIVE), F32),
            pltpu.VMEM((BINS, LIVE), F32),
        ],
        600_000_000,
        8_000_000,
    )(first, count, live, route, features, weights, slots, table, back)


def exchanged(values):
    return lax.all_to_all(values, ("by", "bx"), split_axis=0, concat_axis=0, tiled=True)


def on_device(
    features,
    depth_weight,
    depth_slot,
    patch_count,
    depth_first,
    depth_count,
    tile_dest,
    tile_cells,
    conv_first,
    conv_second,
    grad_out,
):
    by, bx = lax.axis_index("by"), lax.axis_index("bx")
    me = by * lax.axis_size("bx") + bx
    devices = lax.axis_size("by") * lax.axis_size("bx")
    spot = jnp.stack([by, bx]).astype(jnp.int32)
    first_taps = conv_first.reshape(9 * CH, CH)
    second_taps = conv_second.reshape(9 * CH, CH)

    outgoing, table, route = lift(
        depth_first,
        depth_count,
        patch_count,
        tile_dest,
        features,
        depth_weight,
        depth_slot,
        tile_cells,
    )
    arrived = exchanged(outgoing)

    _, edge = lax.optimization_barrier((outgoing, grad_out))
    gout_edges = jnp.stack(
        [
            edge[:2].reshape(80, CH),
            edge[38:].reshape(80, CH),
            edge[:, :2].reshape(80, CH),
            edge[:, 38:].reshape(80, CH),
        ]
    )
    turned_table = jnp.swapaxes(table, 1, 2)
    _, first_late, second_late = lax.optimization_barrier((outgoing, first_taps, second_taps))
    first_flip, second_flip = flipped(first_late, second_late)
    arrived, turned_table, first_flip, second_flip = lax.optimization_barrier(
        (arrived, turned_table, first_flip, second_flip)
    )

    base, top, bottom, left, right = splat(arrived, gout_edges)
    from_left, from_right = shifted(right, "bx", 1), shifted(left, "bx", -1)
    up, down = with_corners(top, bottom, from_left, from_right)
    rims = (shifted(down, "by", 1), shifted(up, "by", -1), from_left, from_right)
    hidden, fcot, sums = activate_tile(
        spot, first_taps, second_flip, base, grad_out.reshape(CELLS, CH), rims
    )
    arrived, sums = lax.optimization_barrier((arrived, sums))
    codes = arrived[:, 128:130, :64].astype(F32)
    cell_column = (codes[:, 0] * 128 + codes[:, 1]).astype(jnp.int32).reshape(-1, 1)
    pairs = [(i, i ^ 1) for i in range(lax.axis_size("bx"))]
    sums = exchanged(sums.reshape(devices, SHARE, 128))
    returning = send_back(first_flip, cell_column, fcot)
    returned = exchanged(add_share(sums, returning))
    out_bev = outward(second_taps, hidden)
    returned, out_bev = lax.optimization_barrier((returned, out_bev))
    own = returned[:, 128:, :]
    other = lax.ppermute(own, "bx", pairs)
    feature_grad, weight_grad = settle(
        depth_first,
        depth_count,
        patch_count,
        route,
        features,
        depth_weight,
        depth_slot,
        turned_table,
        returned,
    )
    other, weight_grad = lax.optimization_barrier((other, weight_grad))
    grad_first, grad_second = widen(spot, own, other)
    return (
        out_bev.reshape(TILE, TILE, CH),
        feature_grad,
        weight_grad,
        grad_first.reshape(3, 3, CH, CH),
        grad_second.reshape(3, 3, CH, CH),
    )


def solution(mesh):
    placed = (
        P(("by", "bx"), None, None),
        P(("by", "bx"), None, None),
        P(("by", "bx"), None, None),
        P(("by", "bx")),
        P(("by", "bx")),
        P(("by", "bx")),
        P(("by", "bx"), None),
        P(("by", "bx"), None),
        P(),
        P(),
        P("by", "bx", None),
    )
    return jax.shard_map(
        on_device,
        mesh=mesh,
        in_specs=placed,
        out_specs=(
            P("by", "bx", None),
            P(("by", "bx"), None, None),
            P(("by", "bx"), None, None),
            P(),
            P(),
        ),
        check_vma=False,
    )
```

```python
from functools import partial

import jax
import jax.numpy as jnp
from jax import lax
from jax.experimental import pallas as pl
from jax.experimental.pallas import tpu as pltpu
from jax.sharding import PartitionSpec as P

CAP = 2
BINS = 64
LIVE = 128
SLOTS = 1024
LIST = 32
LISTS = 32
BLOCKS = 4
CH = 256
TILE = 40
CELLS = TILE * TILE
PITCH = 48
LEAD = 16
FLAT = 2160
WIDE0, WIDE = 48, 2048
CORE0, CORE = 112, 1920
F32 = jnp.float32
BF16 = jnp.bfloat16
VMEM = pl.BlockSpec(memory_space=pltpu.VMEM)
SMEM = pl.BlockSpec(memory_space=pltpu.SMEM)
ANY = pl.BlockSpec(memory_space=pl.ANY)
DMA = pltpu.SemaphoreType.DMA
SENT = 136
SHARE = 72
BACK = 168
PARAMS = pltpu.CompilerParams(vmem_limit_bytes=56 * 1024 * 1024)


def call(kernel, ins, out_shape, out_specs, scratch, flops, moved, **more):
    return pl.pallas_call(
        kernel,
        in_specs=ins,
        out_shape=out_shape,
        out_specs=out_specs,
        scratch_shapes=scratch,
        compiler_params=PARAMS,
        cost_estimate=pl.CostEstimate(flops=flops, bytes_accessed=moved, transcendentals=0),
        **more,
    )


def depth_parts(first_ref, count_ref, weight_ref, b):
    bins = lax.broadcasted_iota(jnp.int32, (BINS, LIVE), 0)
    first = first_ref[b]
    in_range = (bins >= first) & (bins < first + count_ref[b])
    live = jnp.where(in_range, weight_ref[b], 0.0)
    total = jnp.sum(live, axis=0, keepdims=True)
    return in_range, live / total, total


def masked_features(live_ref, feat_ref, b):
    patch = lax.broadcasted_iota(jnp.int32, (LIVE, CH), 0)
    return jnp.where(patch < live_ref[b], feat_ref[b].astype(F32), 0.0).astype(BF16)


def lift_kernel(
    first_ref,
    count_ref,
    live_ref,
    dest_ref,
    feat_ref,
    weight_ref,
    slot_ref,
    cell_ref,
    out_ref,
    table_ref,
    route_ref,
    prob,
    part,
    seen,
    spread_cells,
    code,
):
    def clear(i, c):
        seen[i] = 0
        return c

    lax.fori_loop(0, 128, clear, 0, unroll=8)

    code[...] = jnp.full_like(code, -1)
    quarter = lax.broadcasted_iota(jnp.int32, (8, 128), 1) >> 5
    for k in range(LISTS):
        cells = cell_ref[:, k // 4 * 128 : k // 4 * 128 + 128]
        one = jnp.where(quarter == k % 4, jnp.concatenate([cells, cells], axis=0), 0)
        two = one + pltpu.roll(one, 32, 1)
        spread_cells[k] = two + pltpu.roll(two, 64, 1)
    half = (lax.broadcasted_iota(jnp.int32, (1, 128), 1) >> 5) & 1
    for i in range(BLOCKS * LISTS):
        b, k = i // LISTS, i % LISTS
        tile = dest_ref[b, k]
        rank = seen[tile]
        seen[tile] = rank + 1
        route_ref[i] = tile * CAP + rank
        code[pl.ds(tile, 1), :] = jnp.where(
            half == rank, spread_cells[k, b : b + 1, :], code[pl.ds(tile, 1), :]
        )
    row = lax.broadcasted_iota(jnp.int32, (8, 128), 0)
    high, low = (code[...] >> 7).astype(F32), (code[...] & 127).astype(F32)
    for d in range(128):
        codes = jnp.where(row == 0, high[d : d + 1, :], jnp.where(row == 1, low[d : d + 1, :], 0.0))
        out_ref[d] = jnp.concatenate([jnp.zeros((128, 128), F32), codes], axis=0).astype(BF16)
    low = lax.broadcasted_iota(jnp.int32, (16, LIVE), 0)
    zero = jnp.zeros((), BF16)

    def block(b, c):
        _, share, _ = depth_parts(first_ref, count_ref, weight_ref, b)
        prob[...] = share
        first = first_ref[b]
        quads = (count_ref[b] + 3) // 4
        for chunk in range(4):

            def quad(i, acc):
                mine, high = [], []
                for step in range(4):
                    d = jnp.minimum(first + 4 * i + step, BINS - 1)
                    slot = jnp.broadcast_to(slot_ref[b, pl.ds(d, 1), :], (16, LIVE))
                    share = jnp.broadcast_to(prob[pl.ds(d, 1), :], (16, LIVE))
                    mine.append(jnp.where((slot & 15) == low, share, 0.0).astype(BF16))
                    high.append(((slot >> 4) - chunk * 16).astype(F32).astype(BF16))
                new = []
                for r, a in enumerate(acc):
                    at = jnp.full((), r, BF16)
                    hits = [jnp.where(h == at, m, zero) for h, m in zip(high, mine)]
                    new.append(a + ((hits[0] + hits[1]) + (hits[2] + hits[3])).astype(F32))
                return new

            acc = lax.fori_loop(0, quads, quad, [jnp.zeros((16, LIVE), F32)] * 16)
            table_ref[b, chunk * 256 : (chunk + 1) * 256, :] = jnp.concatenate(acc, axis=0).astype(
                BF16
            )
        part[...] = jnp.dot(
            table_ref[b], masked_features(live_ref, feat_ref, b), preferred_element_type=F32
        ).astype(BF16)
        for k in range(LISTS):
            to = route_ref[b * LISTS + k]
            for h in range(2):
                at = pl.multiple_of((to & 1) * 64 + h * LIST, LIST)
                out_ref[to >> 1, pl.ds(at, LIST), :] = part[
                    k * LIST : (k + 1) * LIST, h * 128 : (h + 1) * 128
                ]
        return c

    lax.fori_loop(0, BLOCKS, block, 0)


def lift(first, count, live, dest, features, weights, slots, cells):
    return call(
        lift_kernel,
        [SMEM] * 4 + [VMEM] * 4,
        (
            jax.ShapeDtypeStruct((128, SENT, 128), BF16),
            jax.ShapeDtypeStruct((BLOCKS, SLOTS, LIVE), BF16),
            jax.ShapeDtypeStruct((BLOCKS * LISTS,), jnp.int32),
        ),
        (VMEM, VMEM, SMEM),
        [
            pltpu.VMEM((BINS, LIVE), F32),
            pltpu.VMEM((SLOTS, CH), BF16),
            pltpu.SMEM((128,), jnp.int32),
            pltpu.VMEM((LISTS, 8, 128), jnp.int32),
            pltpu.VMEM((128, 128), jnp.int32),
        ],
        300_000_000,
        6_000_000,
    )(first, count, live, dest, features, weights, slots, cells)


def splat_kernel(
    list_ref,
    gout_ref,
    base_ref,
    top_ref,
    bottom_ref,
    left_ref,
    right_ref,
    acc,
    hit,
    strip,
    lists,
    code,
):
    rows = 128
    span = 1024
    places = lax.broadcasted_iota(jnp.int32, (rows, span), 0).astype(F32).astype(BF16)
    first_half = lax.broadcasted_iota(jnp.int32, (1, 128), 1) < 64
    one, zero = jnp.ones((), BF16), jnp.zeros((), BF16)
    for n in range(64):
        codes = [list_ref[2 * n + e].astype(F32)[128:, :] for e in range(2)]
        for i in range(2):
            code[n // 8 * 2 + i : n // 8 * 2 + i + 1, n % 8 * 128 : n % 8 * 128 + 128] = jnp.where(
                first_half, codes[0][i : i + 1, :], codes[1][i : i + 1, :]
            )
    for chunk in range(8):
        for n in range(16):
            d = chunk * 16 + n
            for r in range(CAP):
                for h in range(2):
                    at = (n * CAP + r) * LIST
                    lists[at : at + LIST, h * 128 : (h + 1) * 128] = list_ref[
                        d, r * 64 + h * LIST : r * 64 + (h + 1) * LIST, :
                    ]
        high, low = [
            jnp.broadcast_to(code[2 * chunk + i : 2 * chunk + i + 1, :], (rows, span)).astype(BF16)
            for i in range(2)
        ]
        same = jnp.where(low == places, one, zero)
        for m in range(13):
            end = min(rows, CELLS - m * rows)
            hit[m * rows : m * rows + end, :] = jnp.where(
                high == jnp.full((), m, BF16), same, zero
            )[:end, :]
        part = jnp.dot(hit[...], lists[...], preferred_element_type=F32)
        if chunk == 0:
            acc[...] = part
        else:
            acc[...] += part
    base_ref[...] = acc[...].astype(BF16)
    top_ref[:80, :] = acc[:80, :].astype(BF16)
    bottom_ref[:80, :] = acc[CELLS - 80 :, :].astype(BF16)
    for y in range(TILE):
        strip[0, 2 * y : 2 * y + 2, :] = acc[TILE * y : TILE * y + 2, :]
        strip[1, 2 * y : 2 * y + 2, :] = acc[TILE * y + 38 : TILE * y + 40, :]
    left_ref[:80, :] = strip[0].astype(BF16)
    right_ref[:80, :] = strip[1].astype(BF16)
    for n, ref in enumerate((top_ref, bottom_ref, left_ref, right_ref)):
        ref[80:, :] = gout_ref[n]


def splat(lists, gout_edges):
    strip = jax.ShapeDtypeStruct((160, CH), BF16)
    return call(
        splat_kernel,
        [VMEM] * 2,
        (jax.ShapeDtypeStruct((CELLS, CH), BF16),) + (strip,) * 4,
        (VMEM,) * 5,
        [
            pltpu.VMEM((CELLS, CH), F32),
            pltpu.VMEM((CELLS, 1024), BF16),
            pltpu.VMEM((2, 80, CH), F32),
            pltpu.VMEM((1024, CH), BF16),
            pltpu.VMEM((16, 1024), F32),
        ],
        6_700_000_000,
        6_000_000,
    )(lists, gout_edges)


def corner_kernel(top_ref, bottom_ref, left_ref, right_ref, up_ref, down_ref):
    for strip_ref, out_ref, at in ((top_ref, up_ref, 0), (bottom_ref, down_ref, 76)):
        for n in range(2):
            out_ref[96 * n : 96 * n + 80, :] = strip_ref[80 * n : 80 * n + 80, :]
            left = left_ref[80 * n : 80 * n + 80, :].astype(F32)[at : at + 4, :]
            right = right_ref[80 * n : 80 * n + 80, :].astype(F32)[at : at + 4, :]
            out_ref[96 * n + 80 : 96 * n + 96, :] = jnp.concatenate(
                [left, right, jnp.zeros((8, CH), F32)], axis=0
            ).astype(BF16)


def with_corners(top, bottom, left, right):
    strip = jax.ShapeDtypeStruct((192, CH), BF16)
    return call(
        corner_kernel, [VMEM] * 4, (strip, strip), (VMEM, VMEM), [], 1_000_000, 600_000
    )(top, bottom, left, right)


def shifted(values, axis, step):
    count = lax.axis_size(axis)
    return lax.ppermute(
        values, axis, [(i, i + step) for i in range(count) if 0 <= i + step < count]
    )


def lay_out(flat, center, above_ref, below_ref, left_ref, right_ref, n):
    above = above_ref[96 * n : 96 * n + 96, :].astype(F32)
    below = below_ref[96 * n : 96 * n + 96, :].astype(F32)
    left = left_ref[80 * n : 80 * n + 80, :].astype(F32)
    right = right_ref[80 * n : 80 * n + 80, :].astype(F32)
    flat[...] = jnp.zeros_like(flat)

    def spot(y, x):
        return 8 + (y + 2) * PITCH + LEAD + x

    for y in range(TILE):
        flat[spot(y, 0) : spot(y, 0) + TILE, :] = center[y * TILE : (y + 1) * TILE, :].astype(F32)
        flat[spot(y, -2) : spot(y, 0), :] = left[2 * y : 2 * y + 2, :]
        flat[spot(y, 40) : spot(y, 42), :] = right[2 * y : 2 * y + 2, :]
    for r in range(2):
        for rows, y in ((above, r - 2), (below, 40 + r)):
            flat[spot(y, 0) : spot(y, 40), :] = rows[r * TILE : (r + 1) * TILE, :]
            flat[spot(y, -2) : spot(y, 0), :] = rows[80 + 2 * r : 82 + 2 * r, :]
            flat[spot(y, 40) : spot(y, 42), :] = rows[84 + 2 * r : 86 + 2 * r, :]


def spread(flat, wide):
    step = 144
    for at in range(0, FLAT, step):
        for j in range(3):
            wide[at : at + step, j * CH : (j + 1) * CH] = flat[at + 7 + j : at + 7 + j + step, :].astype(
                BF16
            )


def taps(wide, weights, start, rows):
    total = None
    for i in range(3):
        at = pl.multiple_of(start + (i - 1) * PITCH, 16)
        part = jnp.dot(
            wide[pl.ds(at, rows), :],
            weights[i * 3 * CH : (i + 1) * 3 * CH, :],
            preferred_element_type=F32,
        )
        total = part if total is None else total + part
    return total


def flip_kernel(first_ref, second_ref, one_ref, two_ref):
    for source, out in ((first_ref, one_ref), (second_ref, two_ref)):
        for tap in range(9):
            taken = source[(8 - tap) * CH : (9 - tap) * CH, :].astype(F32)
            out[tap * CH : (tap + 1) * CH, :] = taken.T.astype(BF16)


def flipped(first, second):
    out = jax.ShapeDtypeStruct((9 * CH, CH), BF16)
    return call(
        flip_kernel, [VMEM] * 2, (out, out), (VMEM, VMEM), [], 10_000_000, 5_000_000
    )(first, second)


def place_mask(by, bx, start, rows, rim):
    n = lax.broadcasted_iota(jnp.int32, (rows, 128), 0) + (start - LEAD + 1)
    line = (n * 87382) >> 22
    x = n - line * PITCH - 1
    y = line - 2
    near = (y >= -rim) & (y < TILE + rim) & (x >= -rim) & (x < TILE + rim)
    gy, gx = y + by * TILE, x + bx * TILE
    inside = near & (gy >= 0) & (gy < 16 * TILE) & (gx >= 0) & (gx < 8 * TILE)
    return jnp.concatenate([jnp.where(inside, 1.0, 0.0)] * 2, axis=1) > 0.5


def kernel_sums(wide, turned, out):
    for tap in range(9):
        i, j = tap // 3, tap % 3
        at = WIDE0 + (i - 1) * PITCH
        got = jnp.dot(
            turned[...], wide[at : at + WIDE, j * CH : (j + 1) * CH], preferred_element_type=F32
        ).T.astype(BF16)
        for h in range(2):
            to = (2 * tap + h) * CH
            out[to : to + CH, :] = got[:, h * 128 : (h + 1) * 128]


def turn(spot_ref, rows_at, turned):
    for k in range(WIDE // 256):
        at = WIDE0 + k * 256
        inside = place_mask(spot_ref[0], spot_ref[1], at, 256, 0)
        turned[:, k * 256 : (k + 1) * 256] = jnp.where(inside, rows_at(at), 0.0).T.astype(BF16)


def act_kernel(
    spot_ref,
    first_hbm,
    second_hbm,
    base_ref,
    gout_ref,
    above_ref,
    below_ref,
    left_ref,
    right_ref,
    hidden_ref,
    fcot_ref,
    sums_ref,
    first_ref,
    second_ref,
    wide,
    gwide,
    flat,
    flat2,
    turned,
    arrive,
):
    loads = (
        pltpu.make_async_copy(first_hbm, first_ref, arrive.at[0]),
        pltpu.make_async_copy(second_hbm, second_ref, arrive.at[1]),
    )
    for load in loads:
        load.start()
    rims = (above_ref, below_ref, left_ref, right_ref)
    lay_out(flat, base_ref, *rims, 0)
    spread(flat, wide)
    lay_out(flat2, gout_ref, *rims, 1)
    spread(flat2, gwide)
    for values in (flat, flat2):
        values[: WIDE0 + 8, :] = jnp.zeros((WIDE0 + 8, CH), F32)
        values[WIDE0 + 8 + WIDE :, :] = jnp.zeros((FLAT + 8 - WIDE0 - WIDE, CH), F32)
    for load in loads:
        load.wait()

    def activate(k, c):
        at = pl.multiple_of(WIDE0 + k * 512, 16)
        first_act = taps(wide, first_ref, at, 512)
        hidden_cot = taps(gwide, second_ref, at, 512)
        inside = place_mask(spot_ref[0], spot_ref[1], at, 512, 1)
        sig = jax.nn.sigmoid(first_act)
        to = pl.ds(pl.multiple_of(at + 8, 8), 512)
        flat2[to, :] = jnp.where(inside, first_act * sig, 0.0)
        slope = sig * (1.0 + first_act * (1.0 - sig))
        flat[to, :] = jnp.where(inside, hidden_cot * slope, 0.0)
        return c

    lax.fori_loop(0, WIDE // 512, activate, 0)
    fcot_ref[...] = flat[8 : 8 + FLAT, :].astype(BF16)
    hidden_ref[...] = flat2[8 : 8 + FLAT, :].astype(BF16)
    turn(spot_ref, lambda at: flat[at + 8 : at + 264, :], turned)
    kernel_sums(wide, turned, sums_ref.at[0])
    spread(flat2, wide)
    turn(spot_ref, lambda at: gwide[at : at + 256, CH : 2 * CH].astype(F32), turned)
    kernel_sums(wide, turned, sums_ref.at[1])


def activate_tile(spot, first, second, base, gout, rims):
    flat = jax.ShapeDtypeStruct((FLAT, CH), BF16)
    return call(
        act_kernel,
        [SMEM, ANY, ANY] + [VMEM] * 6,
        (flat, flat, jax.ShapeDtypeStruct((2, 18 * CH, 128), BF16)),
        (VMEM,) * 3,
        [
            pltpu.VMEM((9 * CH, CH), BF16),
            pltpu.VMEM((9 * CH, CH), BF16),
            pltpu.VMEM((FLAT, 3 * CH), BF16),
            pltpu.VMEM((FLAT, 3 * CH), BF16),
            pltpu.VMEM((FLAT + 16, CH), F32),
            pltpu.VMEM((FLAT + 16, CH), F32),
            pltpu.VMEM((CH, WIDE), BF16),
            DMA((2,)),
        ],
        9_000_000_000,
        9_000_000,
    )(spot, first, second, base, gout, *rims)


def respread(values_ref, flat, wide):
    flat[...] = jnp.zeros_like(flat)
    flat[8 : 8 + FLAT, :] = values_ref[...].astype(F32)
    spread(flat, wide)


def strip_pads(got, out, k):
    for r in range(5):
        lines = [got[(2 * r + s) * PITCH : (2 * r + s) * PITCH + TILE, :] for s in range(2)]
        to = pl.multiple_of(k * 400 + r * 80, 16)
        out[pl.ds(to, 80), :] = jnp.concatenate(lines, axis=0).astype(BF16)


def back_kernel(first_ref, cell_ref, fcot_ref, out_ref, tile, flat, wide):
    respread(fcot_ref, flat, wide)

    def back(k, c):
        at = pl.multiple_of(CORE0 + k * 480, 16)
        strip_pads(taps(wide, first_ref, at, 480), tile, k)
        return c

    lax.fori_loop(0, 4, back, 0)
    tile[CELLS:, :] = jnp.zeros((1664 - CELLS, CH), BF16)
    places = lax.broadcasted_iota(jnp.int32, (512, 128), 1).astype(F32).astype(BF16)
    one, zero = jnp.ones((), BF16), jnp.zeros((), BF16)

    def pick(k, c):
        at = pl.multiple_of(k * 512, 512)
        cells = jnp.broadcast_to(cell_ref[pl.ds(at, 512), :], (512, 128))
        high = (cells >> 7).astype(F32).astype(BF16)
        same = jnp.where((cells & 127).astype(F32).astype(BF16) == places, one, zero)
        hits = [jnp.where(high == jnp.full((), m, BF16), same, zero) for m in range(13)]
        got = jnp.dot(
            jnp.concatenate(hits, axis=1), tile[...], preferred_element_type=F32
        ).astype(BF16)
        for n in range(16):
            for h in range(2):
                at = (n % 2) * 64 + h * LIST
                out_ref[k * 8 + n // 2, at : at + LIST, :] = got[
                    n * LIST : (n + 1) * LIST, h * 128 : (h + 1) * 128
                ]
        return c

    lax.fori_loop(0, 16, pick, 0)


def send_back(first, cells, fcot):
    return call(
        back_kernel,
        [VMEM] * 3,
        jax.ShapeDtypeStruct((128, BACK, 128), BF16),
        VMEM,
        [
            pltpu.VMEM((1664, CH), BF16),
            pltpu.VMEM((FLAT + 16, CH), F32),
            pltpu.VMEM((FLAT, 3 * CH), BF16),
        ],
        9_000_000_000,
        12_000_000,
    )(first, cells, fcot)


def add_share(parts, back):
    total = jnp.sum(parts.astype(F32), axis=0)
    halves = jnp.stack([total[:40], total[32:]]).astype(BF16)
    beside = jnp.broadcast_to(halves, (64, 2, 40, 128)).reshape(128, 40, 128)
    return lax.dynamic_update_slice(back, beside, (0, 128, 0))


def out_kernel(second_ref, hidden_ref, out_ref, flat, wide):
    respread(hidden_ref, flat, wide)

    def forward(k, c):
        at = pl.multiple_of(CORE0 + k * 480, 16)
        strip_pads(taps(wide, second_ref, at, 480), out_ref, k)
        return c

    lax.fori_loop(0, 4, forward, 0)


def outward(second, hidden_wide):
    return call(
        out_kernel,
        [VMEM] * 2,
        jax.ShapeDtypeStruct((CELLS, CH), BF16),
        VMEM,
        [pltpu.VMEM((FLAT + 16, CH), F32), pltpu.VMEM((FLAT, 3 * CH), BF16)],
        2_300_000_000,
        5_000_000,
    )(second, hidden_wide)


def widen_kernel(spot_ref, own_ref, other_ref, one_hbm, two_hbm, one, two, sent):
    odd = spot_ref[1] % 2 == 1
    copies = [
        pltpu.make_async_copy(wide.at[tap], hbm.at[tap], sent.at[9 * n + tap])
        for n, (wide, hbm) in enumerate(((one, one_hbm), (two, two_hbm)))
        for tap in range(9)
    ]
    for device in range(128):
        own, other = own_ref[device].astype(F32), other_ref[device].astype(F32)
        low, high = jnp.where(odd, other, own), jnp.where(odd, own, other)
        values = jnp.concatenate([low, high[8:, :]], axis=0)
        done = 0
        while done < SHARE:
            part, row = divmod(device * SHARE + done, CH)
            n, part = divmod(part, 18)
            size = min(SHARE - done, CH - row)
            lanes = slice(part % 2 * 128, part % 2 * 128 + 128)
            (one, two)[n][part // 2, row : row + size, lanes] = values[done : done + size, :]
            done += size
            if row + size == CH and part % 2 == 1:
                copies[9 * n + part // 2].start()
    for copy in copies:
        copy.wait()


def widen(spot, own, other):
    out = jax.ShapeDtypeStruct((9, CH, CH), F32)
    wide = pltpu.VMEM((9, CH, CH), F32)
    return call(
        widen_kernel,
        [SMEM, VMEM, VMEM],
        (out, out),
        (ANY, ANY),
        [wide, wide, DMA((18,))],
        1_000_000,
        7_000_000,
    )(spot, own, other)


def settle_kernel(
    first_ref,
    count_ref,
    live_ref,
    route_ref,
    feat_ref,
    weight_ref,
    slot_ref,
    table_ref,
    back_ref,
    gfeat_ref,
    gweight_ref,
    part,
    cot,
    pick,
):
    for b in range(BLOCKS):
        for k in range(LISTS):
            to = route_ref[b * LISTS + k]
            rows = pl.ds(pl.multiple_of((to & 1) * 64, 64), 64)
            part[b * LISTS + k] = back_ref[to >> 1, rows, :]
        got = part[b * LISTS : (b + 1) * LISTS]
        lists = jnp.concatenate(
            [got[:, h * LIST : (h + 1) * LIST, :].reshape(SLOTS, 128) for h in range(2)], axis=1
        )
        masked = masked_features(live_ref, feat_ref, b)
        cot[...] = lax.dot_general(
            lists, masked, (((1,), (1,)), ((), ())), preferred_element_type=F32
        )
        got = jnp.dot(table_ref[b], lists, preferred_element_type=F32)
        patch = lax.broadcasted_iota(jnp.int32, (LIVE, CH), 0)
        gfeat_ref[b] = jnp.where(patch < live_ref[b], got, 0.0).astype(BF16)
        pick[...] = jnp.zeros_like(pick)
        first = first_ref[b]

        def eight(q, c):
            at = pl.multiple_of(q * 8, 8)
            slot = slot_ref[b, pl.ds(at, 8), :]
            low, high = slot & 7, slot >> 3

            def group(g, acc):
                for r in range(16):
                    row = g * 16 + r
                    rows = cot[pl.ds(pl.multiple_of(row * 8, 8), 8), :]
                    found = jnp.take_along_axis(rows, low, axis=0, mode="promise_in_bounds")
                    acc = jnp.where(high == row, found, acc)
                return acc

            pick[pl.ds(at, 8), :] = lax.fori_loop(0, 8, group, jnp.zeros((8, LIVE), F32))
            return c

        lax.fori_loop(first >> 3, (first + count_ref[b] + 7) >> 3, eight, 0)
        in_range, prob, total = depth_parts(first_ref, count_ref, weight_ref, b)
        picked = pick[...]
        mean = jnp.sum(prob * picked, axis=0, keepdims=True)
        gweight_ref[b] = jnp.where(in_range, (picked - mean) / total, 0.0)


def settle(first, count, live, route, features, weights, slots, table, back):
    return call(
        settle_kernel,
        [SMEM] * 4 + [VMEM] * 5,
        (
            jax.ShapeDtypeStruct((BLOCKS, LIVE, CH), BF16),
            jax.ShapeDtypeStruct((BLOCKS, BINS, LIVE), F32),
        ),
        (VMEM, VMEM),
        [
            pltpu.VMEM((BLOCKS * LISTS, CAP * LIST, 128), BF16),
            pltpu.VMEM((SLOTS, LIVE), F32),
            pltpu.VMEM((BINS, LIVE), F32),
        ],
        600_000_000,
        8_000_000,
    )(first, count, live, route, features, weights, slots, table, back)


def exchanged(values):
    return lax.all_to_all(values, ("by", "bx"), split_axis=0, concat_axis=0, tiled=True)


def on_device(
    features,
    depth_weight,
    depth_slot,
    patch_count,
    depth_first,
    depth_count,
    tile_dest,
    tile_cells,
    conv_first,
    conv_second,
    grad_out,
):
    by, bx = lax.axis_index("by"), lax.axis_index("bx")
    me = by * lax.axis_size("bx") + bx
    devices = lax.axis_size("by") * lax.axis_size("bx")
    spot = jnp.stack([by, bx]).astype(jnp.int32)
    first_taps = conv_first.reshape(9 * CH, CH)
    second_taps = conv_second.reshape(9 * CH, CH)

    outgoing, table, route = lift(
        depth_first,
        depth_count,
        patch_count,
        tile_dest,
        features,
        depth_weight,
        depth_slot,
        tile_cells,
    )
    arrived = exchanged(outgoing)

    _, edge = lax.optimization_barrier((outgoing, grad_out))
    gout_edges = jnp.stack(
        [
            edge[:2].reshape(80, CH),
            edge[38:].reshape(80, CH),
            edge[:, :2].reshape(80, CH),
            edge[:, 38:].reshape(80, CH),
        ]
    )
    turned_table = jnp.swapaxes(table, 1, 2)
    _, first_late, second_late = lax.optimization_barrier((outgoing, first_taps, second_taps))
    first_flip, second_flip = flipped(first_late, second_late)
    arrived, turned_table, first_flip, second_flip = lax.optimization_barrier(
        (arrived, turned_table, first_flip, second_flip)
    )

    base, top, bottom, left, right = splat(arrived, gout_edges)
    from_left, from_right = shifted(right, "bx", 1), shifted(left, "bx", -1)
    up, down = with_corners(top, bottom, from_left, from_right)
    rims = (shifted(down, "by", 1), shifted(up, "by", -1), from_left, from_right)
    hidden, fcot, sums = activate_tile(
        spot, first_taps, second_flip, base, grad_out.reshape(CELLS, CH), rims
    )
    arrived, sums = lax.optimization_barrier((arrived, sums))
    codes = arrived[:, 128:130, :64].astype(F32)
    cell_column = (codes[:, 0] * 128 + codes[:, 1]).astype(jnp.int32).reshape(-1, 1)
    pairs = [(i, i ^ 1) for i in range(lax.axis_size("bx"))]
    sums = exchanged(sums.reshape(devices, SHARE, 128))
    returning = send_back(first_flip, cell_column, fcot)
    returned = exchanged(add_share(sums, returning))
    out_bev = outward(second_taps, hidden)
    returned, out_bev = lax.optimization_barrier((returned, out_bev))
    own = returned[:, 128:, :]
    other = lax.ppermute(own, "bx", pairs)
    feature_grad, weight_grad = settle(
        depth_first,
        depth_count,
        patch_count,
        route,
        features,
        depth_weight,
        depth_slot,
        turned_table,
        returned,
    )
    other, weight_grad = lax.optimization_barrier((other, weight_grad))
    grad_first, grad_second = widen(spot, own, other)
    return (
        out_bev.reshape(TILE, TILE, CH),
        feature_grad,
        weight_grad,
        grad_first.reshape(3, 3, CH, CH),
        grad_second.reshape(3, 3, CH, CH),
    )


def solution(mesh):
    placed = (
        P(("by", "bx"), None, None),
        P(("by", "bx"), None, None),
        P(("by", "bx"), None, None),
        P(("by", "bx")),
        P(("by", "bx")),
        P(("by", "bx")),
        P(("by", "bx"), None),
        P(("by", "bx"), None),
        P(),
        P(),
        P("by", "bx", None),
    )
    return jax.shard_map(
        on_device,
        mesh=mesh,
        in_specs=placed,
        out_specs=(
            P("by", "bx", None),
            P(("by", "bx"), None, None),
            P(("by", "bx"), None, None),
            P(),
            P(),
        ),
        check_vma=False,
    )
```

```python
from functools import partial

import jax
import jax.numpy as jnp
from jax import lax
from jax.experimental import pallas as pl
from jax.experimental.pallas import tpu as pltpu
from jax.sharding import PartitionSpec as P

CAP = 2
BINS = 64
LIVE = 128
SLOTS = 1024
LIST = 32
LISTS = 32
BLOCKS = 4
CH = 256
TILE = 40
CELLS = TILE * TILE
PITCH = 48
LEAD = 16
FLAT = 2160
WIDE0, WIDE = 48, 2048
CORE0, CORE = 112, 1920
F32 = jnp.float32
BF16 = jnp.bfloat16
VMEM = pl.BlockSpec(memory_space=pltpu.VMEM)
SMEM = pl.BlockSpec(memory_space=pltpu.SMEM)
ANY = pl.BlockSpec(memory_space=pl.ANY)
DMA = pltpu.SemaphoreType.DMA
SENT = 136
SHARE = 72
BACK = 168
PARAMS = pltpu.CompilerParams(vmem_limit_bytes=56 * 1024 * 1024)


def call(kernel, ins, out_shape, out_specs, scratch, flops, moved, **more):
    return pl.pallas_call(
        kernel,
        in_specs=ins,
        out_shape=out_shape,
        out_specs=out_specs,
        scratch_shapes=scratch,
        compiler_params=PARAMS,
        cost_estimate=pl.CostEstimate(flops=flops, bytes_accessed=moved, transcendentals=0),
        **more,
    )


def depth_parts(first_ref, count_ref, weight_ref, b):
    bins = lax.broadcasted_iota(jnp.int32, (BINS, LIVE), 0)
    first = first_ref[b]
    in_range = (bins >= first) & (bins < first + count_ref[b])
    live = jnp.where(in_range, weight_ref[b], 0.0)
    total = jnp.sum(live, axis=0, keepdims=True)
    return in_range, live / total, total


def masked_features(live_ref, feat_ref, b):
    patch = lax.broadcasted_iota(jnp.int32, (LIVE, CH), 0)
    return jnp.where(patch < live_ref[b], feat_ref[b].astype(F32), 0.0).astype(BF16)


def lift_kernel(
    first_ref,
    count_ref,
    live_ref,
    dest_ref,
    feat_ref,
    weight_ref,
    slot_ref,
    cell_ref,
    out_ref,
    table_ref,
    route_ref,
    prob,
    part,
    seen,
    spread_cells,
    code,
):
    def clear(i, c):
        seen[i] = 0
        return c

    lax.fori_loop(0, 128, clear, 0, unroll=8)

    code[...] = jnp.full_like(code, -1)
    quarter = lax.broadcasted_iota(jnp.int32, (8, 128), 1) >> 5
    for k in range(LISTS):
        cells = cell_ref[:, k // 4 * 128 : k // 4 * 128 + 128]
        one = jnp.where(quarter == k % 4, jnp.concatenate([cells, cells], axis=0), 0)
        two = one + pltpu.roll(one, 32, 1)
        spread_cells[k] = two + pltpu.roll(two, 64, 1)
    half = (lax.broadcasted_iota(jnp.int32, (1, 128), 1) >> 5) & 1
    for i in range(BLOCKS * LISTS):
        b, k = i // LISTS, i % LISTS
        tile = dest_ref[b, k]
        rank = seen[tile]
        seen[tile] = rank + 1
        route_ref[i] = tile * CAP + rank
        code[pl.ds(tile, 1), :] = jnp.where(
            half == rank, spread_cells[k, b : b + 1, :], code[pl.ds(tile, 1), :]
        )
    row = lax.broadcasted_iota(jnp.int32, (8, 128), 0)
    high, low = (code[...] >> 7).astype(F32), (code[...] & 127).astype(F32)
    for d in range(128):
        codes = jnp.where(row == 0, high[d : d + 1, :], jnp.where(row == 1, low[d : d + 1, :], 0.0))
        out_ref[d] = jnp.concatenate([jnp.zeros((128, 128), F32), codes], axis=0).astype(BF16)
    low = lax.broadcasted_iota(jnp.int32, (16, LIVE), 0)
    zero = jnp.zeros((), BF16)

    def block(b, c):
        _, share, _ = depth_parts(first_ref, count_ref, weight_ref, b)
        prob[...] = share
        first = first_ref[b]
        quads = (count_ref[b] + 3) // 4
        for chunk in range(4):

            def quad(i, acc):
                mine, high = [], []
                for step in range(4):
                    d = jnp.minimum(first + 4 * i + step, BINS - 1)
                    slot = jnp.broadcast_to(slot_ref[b, pl.ds(d, 1), :], (16, LIVE))
                    share = jnp.broadcast_to(prob[pl.ds(d, 1), :], (16, LIVE))
                    mine.append(jnp.where((slot & 15) == low, share, 0.0).astype(BF16))
                    high.append(((slot >> 4) - chunk * 16).astype(F32).astype(BF16))
                new = []
                for r, a in enumerate(acc):
                    at = jnp.full((), r, BF16)
                    hits = [jnp.where(h == at, m, zero) for h, m in zip(high, mine)]
                    new.append(a + ((hits[0] + hits[1]) + (hits[2] + hits[3])).astype(F32))
                return new

            acc = lax.fori_loop(0, quads, quad, [jnp.zeros((16, LIVE), F32)] * 16)
            table_ref[b, chunk * 256 : (chunk + 1) * 256, :] = jnp.concatenate(acc, axis=0).astype(
                BF16
            )
        part[...] = jnp.dot(
            table_ref[b], masked_features(live_ref, feat_ref, b), preferred_element_type=F32
        ).astype(BF16)
        for k in range(LISTS):
            to = route_ref[b * LISTS + k]
            for h in range(2):
                at = pl.multiple_of((to & 1) * 64 + h * LIST, LIST)
                out_ref[to >> 1, pl.ds(at, LIST), :] = part[
                    k * LIST : (k + 1) * LIST, h * 128 : (h + 1) * 128
                ]
        return c

    lax.fori_loop(0, BLOCKS, block, 0)


def lift(first, count, live, dest, features, weights, slots, cells):
    return call(
        lift_kernel,
        [SMEM] * 4 + [VMEM] * 4,
        (
            jax.ShapeDtypeStruct((128, SENT, 128), BF16),
            jax.ShapeDtypeStruct((BLOCKS, SLOTS, LIVE), BF16),
            jax.ShapeDtypeStruct((BLOCKS * LISTS,), jnp.int32),
        ),
        (VMEM, VMEM, SMEM),
        [
            pltpu.VMEM((BINS, LIVE), F32),
            pltpu.VMEM((SLOTS, CH), BF16),
            pltpu.SMEM((128,), jnp.int32),
            pltpu.VMEM((LISTS, 8, 128), jnp.int32),
            pltpu.VMEM((128, 128), jnp.int32),
        ],
        300_000_000,
        6_000_000,
    )(first, count, live, dest, features, weights, slots, cells)


def splat_kernel(
    list_ref,
    gout_ref,
    base_ref,
    top_ref,
    bottom_ref,
    left_ref,
    right_ref,
    acc,
    hit,
    strip,
    lists,
    code,
):
    rows = 128
    span = 1024
    places = lax.broadcasted_iota(jnp.int32, (rows, span), 0).astype(F32).astype(BF16)
    first_half = lax.broadcasted_iota(jnp.int32, (1, 128), 1) < 64
    one, zero = jnp.ones((), BF16), jnp.zeros((), BF16)
    for n in range(64):
        codes = [list_ref[2 * n + e].astype(F32)[128:, :] for e in range(2)]
        for i in range(2):
            code[n // 8 * 2 + i : n // 8 * 2 + i + 1, n % 8 * 128 : n % 8 * 128 + 128] = jnp.where(
                first_half, codes[0][i : i + 1, :], codes[1][i : i + 1, :]
            )
    for chunk in range(8):
        for n in range(16):
            d = chunk * 16 + n
            for r in range(CAP):
                for h in range(2):
                    at = (n * CAP + r) * LIST
                    lists[at : at + LIST, h * 128 : (h + 1) * 128] = list_ref[
                        d, r * 64 + h * LIST : r * 64 + (h + 1) * LIST, :
                    ]
        high, low = [
            jnp.broadcast_to(code[2 * chunk + i : 2 * chunk + i + 1, :], (rows, span)).astype(BF16)
            for i in range(2)
        ]
        same = jnp.where(low == places, one, zero)
        for m in range(13):
            end = min(rows, CELLS - m * rows)
            hit[m * rows : m * rows + end, :] = jnp.where(
                high == jnp.full((), m, BF16), same, zero
            )[:end, :]
        part = jnp.dot(hit[...], lists[...], preferred_element_type=F32)
        if chunk == 0:
            acc[...] = part
        else:
            acc[...] += part
    base_ref[...] = acc[...].astype(BF16)
    top_ref[:80, :] = acc[:80, :].astype(BF16)
    bottom_ref[:80, :] = acc[CELLS - 80 :, :].astype(BF16)
    for y in range(TILE):
        strip[0, 2 * y : 2 * y + 2, :] = acc[TILE * y : TILE * y + 2, :]
        strip[1, 2 * y : 2 * y + 2, :] = acc[TILE * y + 38 : TILE * y + 40, :]
    left_ref[:80, :] = strip[0].astype(BF16)
    right_ref[:80, :] = strip[1].astype(BF16)
    for n, ref in enumerate((top_ref, bottom_ref, left_ref, right_ref)):
        ref[80:, :] = gout_ref[n]


def splat(lists, gout_edges):
    strip = jax.ShapeDtypeStruct((160, CH), BF16)
    return call(
        splat_kernel,
        [VMEM] * 2,
        (jax.ShapeDtypeStruct((CELLS, CH), BF16),) + (strip,) * 4,
        (VMEM,) * 5,
        [
            pltpu.VMEM((CELLS, CH), F32),
            pltpu.VMEM((CELLS, 1024), BF16),
            pltpu.VMEM((2, 80, CH), F32),
            pltpu.VMEM((1024, CH), BF16),
            pltpu.VMEM((16, 1024), F32),
        ],
        6_700_000_000,
        6_000_000,
    )(lists, gout_edges)


def corner_kernel(top_ref, bottom_ref, left_ref, right_ref, up_ref, down_ref):
    for strip_ref, out_ref, at in ((top_ref, up_ref, 0), (bottom_ref, down_ref, 76)):
        for n in range(2):
            out_ref[96 * n : 96 * n + 80, :] = strip_ref[80 * n : 80 * n + 80, :]
            left = left_ref[80 * n : 80 * n + 80, :].astype(F32)[at : at + 4, :]
            right = right_ref[80 * n : 80 * n + 80, :].astype(F32)[at : at + 4, :]
            out_ref[96 * n + 80 : 96 * n + 96, :] = jnp.concatenate(
                [left, right, jnp.zeros((8, CH), F32)], axis=0
            ).astype(BF16)


def with_corners(top, bottom, left, right):
    strip = jax.ShapeDtypeStruct((192, CH), BF16)
    return call(
        corner_kernel, [VMEM] * 4, (strip, strip), (VMEM, VMEM), [], 1_000_000, 600_000
    )(top, bottom, left, right)


def shifted(values, axis, step):
    count = lax.axis_size(axis)
    return lax.ppermute(
        values, axis, [(i, i + step) for i in range(count) if 0 <= i + step < count]
    )


def lay_out(flat, center, above_ref, below_ref, left_ref, right_ref, n):
    above = above_ref[96 * n : 96 * n + 96, :].astype(F32)
    below = below_ref[96 * n : 96 * n + 96, :].astype(F32)
    left = left_ref[80 * n : 80 * n + 80, :].astype(F32)
    right = right_ref[80 * n : 80 * n + 80, :].astype(F32)
    flat[...] = jnp.zeros_like(flat)

    def spot(y, x):
        return 8 + (y + 2) * PITCH + LEAD + x

    for y in range(TILE):
        flat[spot(y, 0) : spot(y, 0) + TILE, :] = center[y * TILE : (y + 1) * TILE, :].astype(F32)
        flat[spot(y, -2) : spot(y, 0), :] = left[2 * y : 2 * y + 2, :]
        flat[spot(y, 40) : spot(y, 42), :] = right[2 * y : 2 * y + 2, :]
    for r in range(2):
        for rows, y in ((above, r - 2), (below, 40 + r)):
            flat[spot(y, 0) : spot(y, 40), :] = rows[r * TILE : (r + 1) * TILE, :]
            flat[spot(y, -2) : spot(y, 0), :] = rows[80 + 2 * r : 82 + 2 * r, :]
            flat[spot(y, 40) : spot(y, 42), :] = rows[84 + 2 * r : 86 + 2 * r, :]


def spread(flat, wide):
    step = 144
    for at in range(0, FLAT, step):
        for j in range(3):
            wide[at : at + step, j * CH : (j + 1) * CH] = flat[at + 7 + j : at + 7 + j + step, :].astype(
                BF16
            )


def taps(wide, weights, start, rows):
    total = None
    for i in range(3):
        at = pl.multiple_of(start + (i - 1) * PITCH, 16)
        part = jnp.dot(
            wide[pl.ds(at, rows), :],
            weights[i * 3 * CH : (i + 1) * 3 * CH, :],
            preferred_element_type=F32,
        )
        total = part if total is None else total + part
    return total


def flip_kernel(first_ref, second_ref, one_ref, two_ref):
    for source, out in ((first_ref, one_ref), (second_ref, two_ref)):
        for tap in range(9):
            taken = source[(8 - tap) * CH : (9 - tap) * CH, :].astype(F32)
            out[tap * CH : (tap + 1) * CH, :] = taken.T.astype(BF16)


def flipped(first, second):
    out = jax.ShapeDtypeStruct((9 * CH, CH), BF16)
    return call(
        flip_kernel, [VMEM] * 2, (out, out), (VMEM, VMEM), [], 10_000_000, 5_000_000
    )(first, second)


def place_mask(by, bx, start, rows, rim):
    n = lax.broadcasted_iota(jnp.int32, (rows, 128), 0) + (start - LEAD + 1)
    line = (n * 87382) >> 22
    x = n - line * PITCH - 1
    y = line - 2
    near = (y >= -rim) & (y < TILE + rim) & (x >= -rim) & (x < TILE + rim)
    gy, gx = y + by * TILE, x + bx * TILE
    inside = near & (gy >= 0) & (gy < 16 * TILE) & (gx >= 0) & (gx < 8 * TILE)
    return jnp.concatenate([jnp.where(inside, 1.0, 0.0)] * 2, axis=1) > 0.5


def kernel_sums(wide, turned, out):
    for tap in range(9):
        i, j = tap // 3, tap % 3
        at = WIDE0 + (i - 1) * PITCH
        got = jnp.dot(
            turned[...], wide[at : at + WIDE, j * CH : (j + 1) * CH], preferred_element_type=F32
        ).T.astype(BF16)
        for h in range(2):
            to = (2 * tap + h) * CH
            out[to : to + CH, :] = got[:, h * 128 : (h + 1) * 128]


def turn(spot_ref, rows_at, turned):
    for k in range(WIDE // 256):
        at = WIDE0 + k * 256
        inside = place_mask(spot_ref[0], spot_ref[1], at, 256, 0)
        turned[:, k * 256 : (k + 1) * 256] = jnp.where(inside, rows_at(at), 0.0).T.astype(BF16)


def act_kernel(
    spot_ref,
    first_hbm,
    second_hbm,
    base_ref,
    gout_ref,
    above_ref,
    below_ref,
    left_ref,
    right_ref,
    hidden_ref,
    fcot_ref,
    sums_ref,
    first_ref,
    second_ref,
    wide,
    gwide,
    flat,
    flat2,
    turned,
    arrive,
):
    loads = (
        pltpu.make_async_copy(first_hbm, first_ref, arrive.at[0]),
        pltpu.make_async_copy(second_hbm, second_ref, arrive.at[1]),
    )
    for load in loads:
        load.start()
    rims = (above_ref, below_ref, left_ref, right_ref)
    lay_out(flat, base_ref, *rims, 0)
    spread(flat, wide)
    lay_out(flat2, gout_ref, *rims, 1)
    spread(flat2, gwide)
    for values in (flat, flat2):
        values[: WIDE0 + 8, :] = jnp.zeros((WIDE0 + 8, CH), F32)
        values[WIDE0 + 8 + WIDE :, :] = jnp.zeros((FLAT + 8 - WIDE0 - WIDE, CH), F32)
    for load in loads:
        load.wait()

    def activate(k, c):
        at = pl.multiple_of(WIDE0 + k * 1024, 16)
        first_act = taps(wide, first_ref, at, 1024)
        hidden_cot = taps(gwide, second_ref, at, 1024)
        inside = place_mask(spot_ref[0], spot_ref[1], at, 1024, 1)
        sig = jax.nn.sigmoid(first_act)
        to = pl.ds(pl.multiple_of(at + 8, 8), 1024)
        flat2[to, :] = jnp.where(inside, first_act * sig, 0.0)
        slope = sig * (1.0 + first_act * (1.0 - sig))
        flat[to, :] = jnp.where(inside, hidden_cot * slope, 0.0)
        return c

    lax.fori_loop(0, WIDE // 1024, activate, 0)
    fcot_ref[...] = flat[8 : 8 + FLAT, :].astype(BF16)
    hidden_ref[...] = flat2[8 : 8 + FLAT, :].astype(BF16)
    turn(spot_ref, lambda at: flat[at + 8 : at + 264, :], turned)
    kernel_sums(wide, turned, sums_ref.at[0])
    spread(flat2, wide)
    turn(spot_ref, lambda at: gwide[at : at + 256, CH : 2 * CH].astype(F32), turned)
    kernel_sums(wide, turned, sums_ref.at[1])


def activate_tile(spot, first, second, base, gout, rims):
    flat = jax.ShapeDtypeStruct((FLAT, CH), BF16)
    return call(
        act_kernel,
        [SMEM, ANY, ANY] + [VMEM] * 6,
        (flat, flat, jax.ShapeDtypeStruct((2, 18 * CH, 128), BF16)),
        (VMEM,) * 3,
        [
            pltpu.VMEM((9 * CH, CH), BF16),
            pltpu.VMEM((9 * CH, CH), BF16),
            pltpu.VMEM((FLAT, 3 * CH), BF16),
            pltpu.VMEM((FLAT, 3 * CH), BF16),
            pltpu.VMEM((FLAT + 16, CH), F32),
            pltpu.VMEM((FLAT + 16, CH), F32),
            pltpu.VMEM((CH, WIDE), BF16),
            DMA((2,)),
        ],
        9_000_000_000,
        9_000_000,
    )(spot, first, second, base, gout, *rims)


def respread(values_ref, flat, wide):
    flat[...] = jnp.zeros_like(flat)
    flat[8 : 8 + FLAT, :] = values_ref[...].astype(F32)
    spread(flat, wide)


def strip_pads(got, out, k):
    for r in range(5):
        lines = [got[(2 * r + s) * PITCH : (2 * r + s) * PITCH + TILE, :] for s in range(2)]
        to = pl.multiple_of(k * 400 + r * 80, 16)
        out[pl.ds(to, 80), :] = jnp.concatenate(lines, axis=0).astype(BF16)


def back_kernel(first_ref, cell_ref, fcot_ref, out_ref, tile, flat, wide):
    respread(fcot_ref, flat, wide)

    def back(k, c):
        at = pl.multiple_of(CORE0 + k * 480, 16)
        strip_pads(taps(wide, first_ref, at, 480), tile, k)
        return c

    lax.fori_loop(0, 4, back, 0)
    tile[CELLS:, :] = jnp.zeros((1664 - CELLS, CH), BF16)
    places = lax.broadcasted_iota(jnp.int32, (512, 128), 1).astype(F32).astype(BF16)
    one, zero = jnp.ones((), BF16), jnp.zeros((), BF16)

    def pick(k, c):
        at = pl.multiple_of(k * 512, 512)
        cells = jnp.broadcast_to(cell_ref[pl.ds(at, 512), :], (512, 128))
        high = (cells >> 7).astype(F32).astype(BF16)
        same = jnp.where((cells & 127).astype(F32).astype(BF16) == places, one, zero)
        hits = [jnp.where(high == jnp.full((), m, BF16), same, zero) for m in range(13)]
        got = jnp.dot(
            jnp.concatenate(hits, axis=1), tile[...], preferred_element_type=F32
        ).astype(BF16)
        for n in range(16):
            for h in range(2):
                at = (n % 2) * 64 + h * LIST
                out_ref[k * 8 + n // 2, at : at + LIST, :] = got[
                    n * LIST : (n + 1) * LIST, h * 128 : (h + 1) * 128
                ]
        return c

    lax.fori_loop(0, 16, pick, 0)


def send_back(first, cells, fcot):
    return call(
        back_kernel,
        [VMEM] * 3,
        jax.ShapeDtypeStruct((128, BACK, 128), BF16),
        VMEM,
        [
            pltpu.VMEM((1664, CH), BF16),
            pltpu.VMEM((FLAT + 16, CH), F32),
            pltpu.VMEM((FLAT, 3 * CH), BF16),
        ],
        9_000_000_000,
        12_000_000,
    )(first, cells, fcot)


def add_share(parts, back):
    total = jnp.sum(parts.astype(F32), axis=0)
    halves = jnp.stack([total[:40], total[32:]]).astype(BF16)
    beside = jnp.broadcast_to(halves, (64, 2, 40, 128)).reshape(128, 40, 128)
    return lax.dynamic_update_slice(back, beside, (0, 128, 0))


def out_kernel(second_ref, hidden_ref, out_ref, flat, wide):
    respread(hidden_ref, flat, wide)

    def forward(k, c):
        at = pl.multiple_of(CORE0 + k * 480, 16)
        strip_pads(taps(wide, second_ref, at, 480), out_ref, k)
        return c

    lax.fori_loop(0, 4, forward, 0)


def outward(second, hidden_wide):
    return call(
        out_kernel,
        [VMEM] * 2,
        jax.ShapeDtypeStruct((CELLS, CH), BF16),
        VMEM,
        [pltpu.VMEM((FLAT + 16, CH), F32), pltpu.VMEM((FLAT, 3 * CH), BF16)],
        2_300_000_000,
        5_000_000,
    )(second, hidden_wide)


def widen_kernel(spot_ref, own_ref, other_ref, one_hbm, two_hbm, one, two, sent):
    odd = spot_ref[1] % 2 == 1
    copies = [
        pltpu.make_async_copy(wide.at[tap], hbm.at[tap], sent.at[9 * n + tap])
        for n, (wide, hbm) in enumerate(((one, one_hbm), (two, two_hbm)))
        for tap in range(9)
    ]
    for device in range(128):
        own, other = own_ref[device].astype(F32), other_ref[device].astype(F32)
        low, high = jnp.where(odd, other, own), jnp.where(odd, own, other)
        values = jnp.concatenate([low, high[8:, :]], axis=0)
        done = 0
        while done < SHARE:
            part, row = divmod(device * SHARE + done, CH)
            n, part = divmod(part, 18)
            size = min(SHARE - done, CH - row)
            lanes = slice(part % 2 * 128, part % 2 * 128 + 128)
            (one, two)[n][part // 2, row : row + size, lanes] = values[done : done + size, :]
            done += size
            if row + size == CH and part % 2 == 1:
                copies[9 * n + part // 2].start()
    for copy in copies:
        copy.wait()


def widen(spot, own, other):
    out = jax.ShapeDtypeStruct((9, CH, CH), F32)
    wide = pltpu.VMEM((9, CH, CH), F32)
    return call(
        widen_kernel,
        [SMEM, VMEM, VMEM],
        (out, out),
        (ANY, ANY),
        [wide, wide, DMA((18,))],
        1_000_000,
        7_000_000,
    )(spot, own, other)


def settle_kernel(
    first_ref,
    count_ref,
    live_ref,
    route_ref,
    feat_ref,
    weight_ref,
    slot_ref,
    table_ref,
    back_ref,
    gfeat_ref,
    gweight_ref,
    part,
    cot,
    pick,
):
    for b in range(BLOCKS):
        for k in range(LISTS):
            to = route_ref[b * LISTS + k]
            rows = pl.ds(pl.multiple_of((to & 1) * 64, 64), 64)
            part[b * LISTS + k] = back_ref[to >> 1, rows, :]
        got = part[b * LISTS : (b + 1) * LISTS]
        lists = jnp.concatenate(
            [got[:, h * LIST : (h + 1) * LIST, :].reshape(SLOTS, 128) for h in range(2)], axis=1
        )
        masked = masked_features(live_ref, feat_ref, b)
        cot[...] = lax.dot_general(
            lists, masked, (((1,), (1,)), ((), ())), preferred_element_type=F32
        )
        got = jnp.dot(table_ref[b], lists, preferred_element_type=F32)
        patch = lax.broadcasted_iota(jnp.int32, (LIVE, CH), 0)
        gfeat_ref[b] = jnp.where(patch < live_ref[b], got, 0.0).astype(BF16)
        pick[...] = jnp.zeros_like(pick)
        first = first_ref[b]

        def eight(q, c):
            at = pl.multiple_of(q * 8, 8)
            slot = slot_ref[b, pl.ds(at, 8), :]
            low, high = slot & 7, slot >> 3

            def group(g, acc):
                for r in range(16):
                    row = g * 16 + r
                    rows = cot[pl.ds(pl.multiple_of(row * 8, 8), 8), :]
                    found = jnp.take_along_axis(rows, low, axis=0, mode="promise_in_bounds")
                    acc = jnp.where(high == row, found, acc)
                return acc

            pick[pl.ds(at, 8), :] = lax.fori_loop(
                0, 8, group, jnp.zeros((8, LIVE), F32), unroll=True
            )
            return c

        lax.fori_loop(first >> 3, (first + count_ref[b] + 7) >> 3, eight, 0)
        in_range, prob, total = depth_parts(first_ref, count_ref, weight_ref, b)
        picked = pick[...]
        mean = jnp.sum(prob * picked, axis=0, keepdims=True)
        gweight_ref[b] = jnp.where(in_range, (picked - mean) / total, 0.0)


def settle(first, count, live, route, features, weights, slots, table, back):
    return call(
        settle_kernel,
        [SMEM] * 4 + [VMEM] * 5,
        (
            jax.ShapeDtypeStruct((BLOCKS, LIVE, CH), BF16),
            jax.ShapeDtypeStruct((BLOCKS, BINS, LIVE), F32),
        ),
        (VMEM, VMEM),
        [
            pltpu.VMEM((BLOCKS * LISTS, CAP * LIST, 128), BF16),
            pltpu.VMEM((SLOTS, LIVE), F32),
            pltpu.VMEM((BINS, LIVE), F32),
        ],
        600_000_000,
        8_000_000,
    )(first, count, live, route, features, weights, slots, table, back)


def exchanged(values):
    return lax.all_to_all(values, ("by", "bx"), split_axis=0, concat_axis=0, tiled=True)


def on_device(
    features,
    depth_weight,
    depth_slot,
    patch_count,
    depth_first,
    depth_count,
    tile_dest,
    tile_cells,
    conv_first,
    conv_second,
    grad_out,
):
    by, bx = lax.axis_index("by"), lax.axis_index("bx")
    me = by * lax.axis_size("bx") + bx
    devices = lax.axis_size("by") * lax.axis_size("bx")
    spot = jnp.stack([by, bx]).astype(jnp.int32)
    first_taps = conv_first.reshape(9 * CH, CH)
    second_taps = conv_second.reshape(9 * CH, CH)

    outgoing, table, route = lift(
        depth_first,
        depth_count,
        patch_count,
        tile_dest,
        features,
        depth_weight,
        depth_slot,
        tile_cells,
    )
    arrived = exchanged(outgoing)

    _, edge = lax.optimization_barrier((outgoing, grad_out))
    gout_edges = jnp.stack(
        [
            edge[:2].reshape(80, CH),
            edge[38:].reshape(80, CH),
            edge[:, :2].reshape(80, CH),
            edge[:, 38:].reshape(80, CH),
        ]
    )
    turned_table = jnp.swapaxes(table, 1, 2)
    _, first_late, second_late = lax.optimization_barrier((outgoing, first_taps, second_taps))
    first_flip, second_flip = flipped(first_late, second_late)
    arrived, turned_table, first_flip, second_flip = lax.optimization_barrier(
        (arrived, turned_table, first_flip, second_flip)
    )

    base, top, bottom, left, right = splat(arrived, gout_edges)
    from_left, from_right = shifted(right, "bx", 1), shifted(left, "bx", -1)
    up, down = with_corners(top, bottom, from_left, from_right)
    rims = (shifted(down, "by", 1), shifted(up, "by", -1), from_left, from_right)
    hidden, fcot, sums = activate_tile(
        spot, first_taps, second_flip, base, grad_out.reshape(CELLS, CH), rims
    )
    arrived, sums = lax.optimization_barrier((arrived, sums))
    codes = arrived[:, 128:130, :64].astype(F32)
    cell_column = (codes[:, 0] * 128 + codes[:, 1]).astype(jnp.int32).reshape(-1, 1)
    pairs = [(i, i ^ 1) for i in range(lax.axis_size("bx"))]
    sums = exchanged(sums.reshape(devices, SHARE, 128))
    returning = send_back(first_flip, cell_column, fcot)
    returned = exchanged(add_share(sums, returning))
    out_bev = outward(second_taps, hidden)
    returned, out_bev = lax.optimization_barrier((returned, out_bev))
    own = returned[:, 128:, :]
    other = lax.ppermute(own, "bx", pairs)
    feature_grad, weight_grad = settle(
        depth_first,
        depth_count,
        patch_count,
        route,
        features,
        depth_weight,
        depth_slot,
        turned_table,
        returned,
    )
    other, weight_grad = lax.optimization_barrier((other, weight_grad))
    grad_first, grad_second = widen(spot, own, other)
    return (
        out_bev.reshape(TILE, TILE, CH),
        feature_grad,
        weight_grad,
        grad_first.reshape(3, 3, CH, CH),
        grad_second.reshape(3, 3, CH, CH),
    )


def solution(mesh):
    placed = (
        P(("by", "bx"), None, None),
        P(("by", "bx"), None, None),
        P(("by", "bx"), None, None),
        P(("by", "bx")),
        P(("by", "bx")),
        P(("by", "bx")),
        P(("by", "bx"), None),
        P(("by", "bx"), None),
        P(),
        P(),
        P("by", "bx", None),
    )
    return jax.shard_map(
        on_device,
        mesh=mesh,
        in_specs=placed,
        out_specs=(
            P("by", "bx", None),
            P(("by", "bx"), None, None),
            P(("by", "bx"), None, None),
            P(),
            P(),
        ),
        check_vma=False,
    )
```

```python
from functools import partial

import jax
import jax.numpy as jnp
from jax import lax
from jax.experimental import pallas as pl
from jax.experimental.pallas import tpu as pltpu
from jax.sharding import PartitionSpec as P

CAP = 2
BINS = 64
LIVE = 128
SLOTS = 1024
LIST = 32
LISTS = 32
BLOCKS = 4
CH = 256
TILE = 40
CELLS = TILE * TILE
PITCH = 48
LEAD = 16
FLAT = 2160
WIDE0, WIDE = 48, 2048
CORE0, CORE = 112, 1920
F32 = jnp.float32
BF16 = jnp.bfloat16
VMEM = pl.BlockSpec(memory_space=pltpu.VMEM)
SMEM = pl.BlockSpec(memory_space=pltpu.SMEM)
ANY = pl.BlockSpec(memory_space=pl.ANY)
DMA = pltpu.SemaphoreType.DMA
SENT = 136
SHARE = 72
BACK = 168
PARAMS = pltpu.CompilerParams(vmem_limit_bytes=56 * 1024 * 1024)


def call(kernel, ins, out_shape, out_specs, scratch, flops, moved, **more):
    return pl.pallas_call(
        kernel,
        in_specs=ins,
        out_shape=out_shape,
        out_specs=out_specs,
        scratch_shapes=scratch,
        compiler_params=PARAMS,
        cost_estimate=pl.CostEstimate(flops=flops, bytes_accessed=moved, transcendentals=0),
        **more,
    )


def depth_parts(first_ref, count_ref, weight_ref, b):
    bins = lax.broadcasted_iota(jnp.int32, (BINS, LIVE), 0)
    first = first_ref[b]
    in_range = (bins >= first) & (bins < first + count_ref[b])
    live = jnp.where(in_range, weight_ref[b], 0.0)
    total = jnp.sum(live, axis=0, keepdims=True)
    return in_range, live / total, total


def masked_features(live_ref, feat_ref, b):
    patch = lax.broadcasted_iota(jnp.int32, (LIVE, CH), 0)
    return jnp.where(patch < live_ref[b], feat_ref[b].astype(F32), 0.0).astype(BF16)


def lift_kernel(
    first_ref,
    count_ref,
    live_ref,
    dest_ref,
    feat_ref,
    weight_ref,
    slot_ref,
    cell_ref,
    out_ref,
    table_ref,
    route_ref,
    prob,
    part,
    seen,
    spread_cells,
    code,
):
    def clear(i, c):
        seen[i] = 0
        return c

    lax.fori_loop(0, 128, clear, 0, unroll=8)

    code[...] = jnp.full_like(code, -1)
    quarter = lax.broadcasted_iota(jnp.int32, (8, 128), 1) >> 5
    for k in range(LISTS):
        cells = cell_ref[:, k // 4 * 128 : k // 4 * 128 + 128]
        one = jnp.where(quarter == k % 4, jnp.concatenate([cells, cells], axis=0), 0)
        two = one + pltpu.roll(one, 32, 1)
        spread_cells[k] = two + pltpu.roll(two, 64, 1)
    half = (lax.broadcasted_iota(jnp.int32, (1, 128), 1) >> 5) & 1
    for i in range(BLOCKS * LISTS):
        b, k = i // LISTS, i % LISTS
        tile = dest_ref[b, k]
        rank = seen[tile]
        seen[tile] = rank + 1
        route_ref[i] = tile * CAP + rank
        code[pl.ds(tile, 1), :] = jnp.where(
            half == rank, spread_cells[k, b : b + 1, :], code[pl.ds(tile, 1), :]
        )
    row = lax.broadcasted_iota(jnp.int32, (8, 128), 0)
    high, low = (code[...] >> 7).astype(F32), (code[...] & 127).astype(F32)
    for d in range(128):
        codes = jnp.where(row == 0, high[d : d + 1, :], jnp.where(row == 1, low[d : d + 1, :], 0.0))
        out_ref[d] = jnp.concatenate([jnp.zeros((128, 128), F32), codes], axis=0).astype(BF16)
    low = lax.broadcasted_iota(jnp.int32, (16, LIVE), 0)
    zero = jnp.zeros((), BF16)

    def block(b, c):
        _, share, _ = depth_parts(first_ref, count_ref, weight_ref, b)
        prob[...] = share
        first = first_ref[b]
        quads = (count_ref[b] + 3) // 4
        for chunk in range(4):

            def quad(i, acc):
                mine, high = [], []
                for step in range(4):
                    d = jnp.minimum(first + 4 * i + step, BINS - 1)
                    slot = jnp.broadcast_to(slot_ref[b, pl.ds(d, 1), :], (16, LIVE))
                    share = jnp.broadcast_to(prob[pl.ds(d, 1), :], (16, LIVE))
                    mine.append(jnp.where((slot & 15) == low, share, 0.0).astype(BF16))
                    high.append(((slot >> 4) - chunk * 16).astype(F32).astype(BF16))
                new = []
                for r, a in enumerate(acc):
                    at = jnp.full((), r, BF16)
                    hits = [jnp.where(h == at, m, zero) for h, m in zip(high, mine)]
                    new.append(a + ((hits[0] + hits[1]) + (hits[2] + hits[3])).astype(F32))
                return new

            acc = lax.fori_loop(0, quads, quad, [jnp.zeros((16, LIVE), F32)] * 16)
            table_ref[b, chunk * 256 : (chunk + 1) * 256, :] = jnp.concatenate(acc, axis=0).astype(
                BF16
            )
        part[...] = jnp.dot(
            table_ref[b], masked_features(live_ref, feat_ref, b), preferred_element_type=F32
        ).astype(BF16)
        for k in range(LISTS):
            to = route_ref[b * LISTS + k]
            for h in range(2):
                at = pl.multiple_of((to & 1) * 64 + h * LIST, LIST)
                out_ref[to >> 1, pl.ds(at, LIST), :] = part[
                    k * LIST : (k + 1) * LIST, h * 128 : (h + 1) * 128
                ]
        return c

    lax.fori_loop(0, BLOCKS, block, 0, unroll=True)


def lift(first, count, live, dest, features, weights, slots, cells):
    return call(
        lift_kernel,
        [SMEM] * 4 + [VMEM] * 4,
        (
            jax.ShapeDtypeStruct((128, SENT, 128), BF16),
            jax.ShapeDtypeStruct((BLOCKS, SLOTS, LIVE), BF16),
            jax.ShapeDtypeStruct((BLOCKS * LISTS,), jnp.int32),
        ),
        (VMEM, VMEM, SMEM),
        [
            pltpu.VMEM((BINS, LIVE), F32),
            pltpu.VMEM((SLOTS, CH), BF16),
            pltpu.SMEM((128,), jnp.int32),
            pltpu.VMEM((LISTS, 8, 128), jnp.int32),
            pltpu.VMEM((128, 128), jnp.int32),
        ],
        300_000_000,
        6_000_000,
    )(first, count, live, dest, features, weights, slots, cells)


def splat_kernel(
    list_ref,
    gout_ref,
    base_ref,
    top_ref,
    bottom_ref,
    left_ref,
    right_ref,
    acc,
    hit,
    strip,
    lists,
    code,
):
    rows = 128
    span = 1024
    places = lax.broadcasted_iota(jnp.int32, (rows, span), 0).astype(F32).astype(BF16)
    first_half = lax.broadcasted_iota(jnp.int32, (1, 128), 1) < 64
    one, zero = jnp.ones((), BF16), jnp.zeros((), BF16)
    for n in range(64):
        codes = [list_ref[2 * n + e].astype(F32)[128:, :] for e in range(2)]
        for i in range(2):
            code[n // 8 * 2 + i : n // 8 * 2 + i + 1, n % 8 * 128 : n % 8 * 128 + 128] = jnp.where(
                first_half, codes[0][i : i + 1, :], codes[1][i : i + 1, :]
            )
    for chunk in range(8):
        for n in range(16):
            d = chunk * 16 + n
            for r in range(CAP):
                for h in range(2):
                    at = (n * CAP + r) * LIST
                    lists[at : at + LIST, h * 128 : (h + 1) * 128] = list_ref[
                        d, r * 64 + h * LIST : r * 64 + (h + 1) * LIST, :
                    ]
        high, low = [
            jnp.broadcast_to(code[2 * chunk + i : 2 * chunk + i + 1, :], (rows, span)).astype(BF16)
            for i in range(2)
        ]
        same = jnp.where(low == places, one, zero)
        for m in range(13):
            end = min(rows, CELLS - m * rows)
            hit[m * rows : m * rows + end, :] = jnp.where(
                high == jnp.full((), m, BF16), same, zero
            )[:end, :]
        part = jnp.dot(hit[...], lists[...], preferred_element_type=F32)
        if chunk == 0:
            acc[...] = part
        else:
            acc[...] += part
    base_ref[...] = acc[...].astype(BF16)
    top_ref[:80, :] = acc[:80, :].astype(BF16)
    bottom_ref[:80, :] = acc[CELLS - 80 :, :].astype(BF16)
    for y in range(TILE):
        strip[0, 2 * y : 2 * y + 2, :] = acc[TILE * y : TILE * y + 2, :]
        strip[1, 2 * y : 2 * y + 2, :] = acc[TILE * y + 38 : TILE * y + 40, :]
    left_ref[:80, :] = strip[0].astype(BF16)
    right_ref[:80, :] = strip[1].astype(BF16)
    for n, ref in enumerate((top_ref, bottom_ref, left_ref, right_ref)):
        ref[80:, :] = gout_ref[n]


def splat(lists, gout_edges):
    strip = jax.ShapeDtypeStruct((160, CH), BF16)
    return call(
        splat_kernel,
        [VMEM] * 2,
        (jax.ShapeDtypeStruct((CELLS, CH), BF16),) + (strip,) * 4,
        (VMEM,) * 5,
        [
            pltpu.VMEM((CELLS, CH), F32),
            pltpu.VMEM((CELLS, 1024), BF16),
            pltpu.VMEM((2, 80, CH), F32),
            pltpu.VMEM((1024, CH), BF16),
            pltpu.VMEM((16, 1024), F32),
        ],
        6_700_000_000,
        6_000_000,
    )(lists, gout_edges)


def corner_kernel(top_ref, bottom_ref, left_ref, right_ref, up_ref, down_ref):
    for strip_ref, out_ref, at in ((top_ref, up_ref, 0), (bottom_ref, down_ref, 76)):
        for n in range(2):
            out_ref[96 * n : 96 * n + 80, :] = strip_ref[80 * n : 80 * n + 80, :]
            left = left_ref[80 * n : 80 * n + 80, :].astype(F32)[at : at + 4, :]
            right = right_ref[80 * n : 80 * n + 80, :].astype(F32)[at : at + 4, :]
            out_ref[96 * n + 80 : 96 * n + 96, :] = jnp.concatenate(
                [left, right, jnp.zeros((8, CH), F32)], axis=0
            ).astype(BF16)


def with_corners(top, bottom, left, right):
    strip = jax.ShapeDtypeStruct((192, CH), BF16)
    return call(
        corner_kernel, [VMEM] * 4, (strip, strip), (VMEM, VMEM), [], 1_000_000, 600_000
    )(top, bottom, left, right)


def shifted(values, axis, step):
    count = lax.axis_size(axis)
    return lax.ppermute(
        values, axis, [(i, i + step) for i in range(count) if 0 <= i + step < count]
    )


def lay_out(flat, center, above_ref, below_ref, left_ref, right_ref, n):
    above = above_ref[96 * n : 96 * n + 96, :].astype(F32)
    below = below_ref[96 * n : 96 * n + 96, :].astype(F32)
    left = left_ref[80 * n : 80 * n + 80, :].astype(F32)
    right = right_ref[80 * n : 80 * n + 80, :].astype(F32)
    flat[...] = jnp.zeros_like(flat)

    def spot(y, x):
        return 8 + (y + 2) * PITCH + LEAD + x

    for y in range(TILE):
        flat[spot(y, 0) : spot(y, 0) + TILE, :] = center[y * TILE : (y + 1) * TILE, :].astype(F32)
        flat[spot(y, -2) : spot(y, 0), :] = left[2 * y : 2 * y + 2, :]
        flat[spot(y, 40) : spot(y, 42), :] = right[2 * y : 2 * y + 2, :]
    for r in range(2):
        for rows, y in ((above, r - 2), (below, 40 + r)):
            flat[spot(y, 0) : spot(y, 40), :] = rows[r * TILE : (r + 1) * TILE, :]
            flat[spot(y, -2) : spot(y, 0), :] = rows[80 + 2 * r : 82 + 2 * r, :]
            flat[spot(y, 40) : spot(y, 42), :] = rows[84 + 2 * r : 86 + 2 * r, :]


def spread(flat, wide):
    step = 144
    for at in range(0, FLAT, step):
        for j in range(3):
            wide[at : at + step, j * CH : (j + 1) * CH] = flat[at + 7 + j : at + 7 + j + step, :].astype(
                BF16
            )


def taps(wide, weights, start, rows):
    total = None
    for i in range(3):
        at = pl.multiple_of(start + (i - 1) * PITCH, 16)
        part = jnp.dot(
            wide[pl.ds(at, rows), :],
            weights[i * 3 * CH : (i + 1) * 3 * CH, :],
            preferred_element_type=F32,
        )
        total = part if total is None else total + part
    return total


def flip_kernel(first_ref, second_ref, one_ref, two_ref):
    for source, out in ((first_ref, one_ref), (second_ref, two_ref)):
        for tap in range(9):
            taken = source[(8 - tap) * CH : (9 - tap) * CH, :].astype(F32)
            out[tap * CH : (tap + 1) * CH, :] = taken.T.astype(BF16)


def flipped(first, second):
    out = jax.ShapeDtypeStruct((9 * CH, CH), BF16)
    return call(
        flip_kernel, [VMEM] * 2, (out, out), (VMEM, VMEM), [], 10_000_000, 5_000_000
    )(first, second)


def place_mask(by, bx, start, rows, rim):
    n = lax.broadcasted_iota(jnp.int32, (rows, 128), 0) + (start - LEAD + 1)
    line = (n * 87382) >> 22
    x = n - line * PITCH - 1
    y = line - 2
    near = (y >= -rim) & (y < TILE + rim) & (x >= -rim) & (x < TILE + rim)
    gy, gx = y + by * TILE, x + bx * TILE
    inside = near & (gy >= 0) & (gy < 16 * TILE) & (gx >= 0) & (gx < 8 * TILE)
    return jnp.concatenate([jnp.where(inside, 1.0, 0.0)] * 2, axis=1) > 0.5


def kernel_sums(wide, turned, out):
    for tap in range(9):
        i, j = tap // 3, tap % 3
        at = WIDE0 + (i - 1) * PITCH
        got = jnp.dot(
            turned[...], wide[at : at + WIDE, j * CH : (j + 1) * CH], preferred_element_type=F32
        ).T.astype(BF16)
        for h in range(2):
            to = (2 * tap + h) * CH
            out[to : to + CH, :] = got[:, h * 128 : (h + 1) * 128]


def turn(spot_ref, rows_at, turned):
    for k in range(WIDE // 256):
        at = WIDE0 + k * 256
        inside = place_mask(spot_ref[0], spot_ref[1], at, 256, 0)
        turned[:, k * 256 : (k + 1) * 256] = jnp.where(inside, rows_at(at), 0.0).T.astype(BF16)


def act_kernel(
    spot_ref,
    first_hbm,
    second_hbm,
    base_ref,
    gout_ref,
    above_ref,
    below_ref,
    left_ref,
    right_ref,
    hidden_ref,
    fcot_ref,
    sums_ref,
    first_ref,
    second_ref,
    wide,
    gwide,
    flat,
    flat2,
    turned,
    arrive,
):
    loads = (
        pltpu.make_async_copy(first_hbm, first_ref, arrive.at[0]),
        pltpu.make_async_copy(second_hbm, second_ref, arrive.at[1]),
    )
    for load in loads:
        load.start()
    rims = (above_ref, below_ref, left_ref, right_ref)
    lay_out(flat, base_ref, *rims, 0)
    spread(flat, wide)
    lay_out(flat2, gout_ref, *rims, 1)
    spread(flat2, gwide)
    for values in (flat, flat2):
        values[: WIDE0 + 8, :] = jnp.zeros((WIDE0 + 8, CH), F32)
        values[WIDE0 + 8 + WIDE :, :] = jnp.zeros((FLAT + 8 - WIDE0 - WIDE, CH), F32)
    for load in loads:
        load.wait()

    def activate(k, c):
        at = pl.multiple_of(WIDE0 + k * 1024, 16)
        first_act = taps(wide, first_ref, at, 1024)
        hidden_cot = taps(gwide, second_ref, at, 1024)
        inside = place_mask(spot_ref[0], spot_ref[1], at, 1024, 1)
        sig = jax.nn.sigmoid(first_act)
        to = pl.ds(pl.multiple_of(at + 8, 8), 1024)
        flat2[to, :] = jnp.where(inside, first_act * sig, 0.0)
        slope = sig * (1.0 + first_act * (1.0 - sig))
        flat[to, :] = jnp.where(inside, hidden_cot * slope, 0.0)
        return c

    lax.fori_loop(0, WIDE // 1024, activate, 0)
    fcot_ref[...] = flat[8 : 8 + FLAT, :].astype(BF16)
    hidden_ref[...] = flat2[8 : 8 + FLAT, :].astype(BF16)
    turn(spot_ref, lambda at: flat[at + 8 : at + 264, :], turned)
    kernel_sums(wide, turned, sums_ref.at[0])
    spread(flat2, wide)
    turn(spot_ref, lambda at: gwide[at : at + 256, CH : 2 * CH].astype(F32), turned)
    kernel_sums(wide, turned, sums_ref.at[1])


def activate_tile(spot, first, second, base, gout, rims):
    flat = jax.ShapeDtypeStruct((FLAT, CH), BF16)
    return call(
        act_kernel,
        [SMEM, ANY, ANY] + [VMEM] * 6,
        (flat, flat, jax.ShapeDtypeStruct((2, 18 * CH, 128), BF16)),
        (VMEM,) * 3,
        [
            pltpu.VMEM((9 * CH, CH), BF16),
            pltpu.VMEM((9 * CH, CH), BF16),
            pltpu.VMEM((FLAT, 3 * CH), BF16),
            pltpu.VMEM((FLAT, 3 * CH), BF16),
            pltpu.VMEM((FLAT + 16, CH), F32),
            pltpu.VMEM((FLAT + 16, CH), F32),
            pltpu.VMEM((CH, WIDE), BF16),
            DMA((2,)),
        ],
        9_000_000_000,
        9_000_000,
    )(spot, first, second, base, gout, *rims)


def respread(values_ref, flat, wide):
    flat[...] = jnp.zeros_like(flat)
    flat[8 : 8 + FLAT, :] = values_ref[...].astype(F32)
    spread(flat, wide)


def strip_pads(got, out, k):
    for r in range(5):
        lines = [got[(2 * r + s) * PITCH : (2 * r + s) * PITCH + TILE, :] for s in range(2)]
        to = pl.multiple_of(k * 400 + r * 80, 16)
        out[pl.ds(to, 80), :] = jnp.concatenate(lines, axis=0).astype(BF16)


def back_kernel(first_ref, cell_ref, fcot_ref, out_ref, tile, flat, wide):
    respread(fcot_ref, flat, wide)

    def back(k, c):
        at = pl.multiple_of(CORE0 + k * 480, 16)
        strip_pads(taps(wide, first_ref, at, 480), tile, k)
        return c

    lax.fori_loop(0, 4, back, 0)
    tile[CELLS:, :] = jnp.zeros((1664 - CELLS, CH), BF16)
    places = lax.broadcasted_iota(jnp.int32, (512, 128), 1).astype(F32).astype(BF16)
    one, zero = jnp.ones((), BF16), jnp.zeros((), BF16)

    def pick(k, c):
        at = pl.multiple_of(k * 512, 512)
        cells = jnp.broadcast_to(cell_ref[pl.ds(at, 512), :], (512, 128))
        high = (cells >> 7).astype(F32).astype(BF16)
        same = jnp.where((cells & 127).astype(F32).astype(BF16) == places, one, zero)
        hits = [jnp.where(high == jnp.full((), m, BF16), same, zero) for m in range(13)]
        got = jnp.dot(
            jnp.concatenate(hits, axis=1), tile[...], preferred_element_type=F32
        ).astype(BF16)
        for n in range(16):
            for h in range(2):
                at = (n % 2) * 64 + h * LIST
                out_ref[k * 8 + n // 2, at : at + LIST, :] = got[
                    n * LIST : (n + 1) * LIST, h * 128 : (h + 1) * 128
                ]
        return c

    lax.fori_loop(0, 16, pick, 0)


def send_back(first, cells, fcot):
    return call(
        back_kernel,
        [VMEM] * 3,
        jax.ShapeDtypeStruct((128, BACK, 128), BF16),
        VMEM,
        [
            pltpu.VMEM((1664, CH), BF16),
            pltpu.VMEM((FLAT + 16, CH), F32),
            pltpu.VMEM((FLAT, 3 * CH), BF16),
        ],
        9_000_000_000,
        12_000_000,
    )(first, cells, fcot)


def add_share(parts, back):
    total = jnp.sum(parts.astype(F32), axis=0)
    halves = jnp.stack([total[:40], total[32:]]).astype(BF16)
    beside = jnp.broadcast_to(halves, (64, 2, 40, 128)).reshape(128, 40, 128)
    return lax.dynamic_update_slice(back, beside, (0, 128, 0))


def out_kernel(second_ref, hidden_ref, out_ref, flat, wide):
    respread(hidden_ref, flat, wide)

    def forward(k, c):
        at = pl.multiple_of(CORE0 + k * 480, 16)
        strip_pads(taps(wide, second_ref, at, 480), out_ref, k)
        return c

    lax.fori_loop(0, 4, forward, 0)


def outward(second, hidden_wide):
    return call(
        out_kernel,
        [VMEM] * 2,
        jax.ShapeDtypeStruct((CELLS, CH), BF16),
        VMEM,
        [pltpu.VMEM((FLAT + 16, CH), F32), pltpu.VMEM((FLAT, 3 * CH), BF16)],
        2_300_000_000,
        5_000_000,
    )(second, hidden_wide)


def widen_kernel(spot_ref, own_ref, other_ref, one_hbm, two_hbm, one, two, sent):
    odd = spot_ref[1] % 2 == 1
    copies = [
        pltpu.make_async_copy(wide.at[tap], hbm.at[tap], sent.at[9 * n + tap])
        for n, (wide, hbm) in enumerate(((one, one_hbm), (two, two_hbm)))
        for tap in range(9)
    ]
    for device in range(128):
        own, other = own_ref[device].astype(F32), other_ref[device].astype(F32)
        low, high = jnp.where(odd, other, own), jnp.where(odd, own, other)
        values = jnp.concatenate([low, high[8:, :]], axis=0)
        done = 0
        while done < SHARE:
            part, row = divmod(device * SHARE + done, CH)
            n, part = divmod(part, 18)
            size = min(SHARE - done, CH - row)
            lanes = slice(part % 2 * 128, part % 2 * 128 + 128)
            (one, two)[n][part // 2, row : row + size, lanes] = values[done : done + size, :]
            done += size
            if row + size == CH and part % 2 == 1:
                copies[9 * n + part // 2].start()
    for copy in copies:
        copy.wait()


def widen(spot, own, other):
    out = jax.ShapeDtypeStruct((9, CH, CH), F32)
    wide = pltpu.VMEM((9, CH, CH), F32)
    return call(
        widen_kernel,
        [SMEM, VMEM, VMEM],
        (out, out),
        (ANY, ANY),
        [wide, wide, DMA((18,))],
        1_000_000,
        7_000_000,
    )(spot, own, other)


def settle_kernel(
    first_ref,
    count_ref,
    live_ref,
    route_ref,
    feat_ref,
    weight_ref,
    slot_ref,
    table_ref,
    back_ref,
    gfeat_ref,
    gweight_ref,
    part,
    cot,
    pick,
):
    for b in range(BLOCKS):
        for k in range(LISTS):
            to = route_ref[b * LISTS + k]
            rows = pl.ds(pl.multiple_of((to & 1) * 64, 64), 64)
            part[b * LISTS + k] = back_ref[to >> 1, rows, :]
        got = part[b * LISTS : (b + 1) * LISTS]
        lists = jnp.concatenate(
            [got[:, h * LIST : (h + 1) * LIST, :].reshape(SLOTS, 128) for h in range(2)], axis=1
        )
        masked = masked_features(live_ref, feat_ref, b)
        cot[...] = lax.dot_general(
            lists, masked, (((1,), (1,)), ((), ())), preferred_element_type=F32
        )
        got = jnp.dot(table_ref[b], lists, preferred_element_type=F32)
        patch = lax.broadcasted_iota(jnp.int32, (LIVE, CH), 0)
        gfeat_ref[b] = jnp.where(patch < live_ref[b], got, 0.0).astype(BF16)
        pick[...] = jnp.zeros_like(pick)
        first = first_ref[b]

        def eight(q, c):
            at = pl.multiple_of(q * 8, 8)
            slot = slot_ref[b, pl.ds(at, 8), :]
            low, high = slot & 7, slot >> 3

            def group(g, acc):
                for r in range(16):
                    row = g * 16 + r
                    rows = cot[pl.ds(pl.multiple_of(row * 8, 8), 8), :]
                    found = jnp.take_along_axis(rows, low, axis=0, mode="promise_in_bounds")
                    acc = jnp.where(high == row, found, acc)
                return acc

            pick[pl.ds(at, 8), :] = lax.fori_loop(
                0, 8, group, jnp.zeros((8, LIVE), F32), unroll=True
            )
            return c

        lax.fori_loop(first >> 3, (first + count_ref[b] + 7) >> 3, eight, 0)
        in_range, prob, total = depth_parts(first_ref, count_ref, weight_ref, b)
        picked = pick[...]
        mean = jnp.sum(prob * picked, axis=0, keepdims=True)
        gweight_ref[b] = jnp.where(in_range, (picked - mean) / total, 0.0)


def settle(first, count, live, route, features, weights, slots, table, back):
    return call(
        settle_kernel,
        [SMEM] * 4 + [VMEM] * 5,
        (
            jax.ShapeDtypeStruct((BLOCKS, LIVE, CH), BF16),
            jax.ShapeDtypeStruct((BLOCKS, BINS, LIVE), F32),
        ),
        (VMEM, VMEM),
        [
            pltpu.VMEM((BLOCKS * LISTS, CAP * LIST, 128), BF16),
            pltpu.VMEM((SLOTS, LIVE), F32),
            pltpu.VMEM((BINS, LIVE), F32),
        ],
        600_000_000,
        8_000_000,
    )(first, count, live, route, features, weights, slots, table, back)


def exchanged(values):
    return lax.all_to_all(values, ("by", "bx"), split_axis=0, concat_axis=0, tiled=True)


def on_device(
    features,
    depth_weight,
    depth_slot,
    patch_count,
    depth_first,
    depth_count,
    tile_dest,
    tile_cells,
    conv_first,
    conv_second,
    grad_out,
):
    by, bx = lax.axis_index("by"), lax.axis_index("bx")
    me = by * lax.axis_size("bx") + bx
    devices = lax.axis_size("by") * lax.axis_size("bx")
    spot = jnp.stack([by, bx]).astype(jnp.int32)
    first_taps = conv_first.reshape(9 * CH, CH)
    second_taps = conv_second.reshape(9 * CH, CH)

    outgoing, table, route = lift(
        depth_first,
        depth_count,
        patch_count,
        tile_dest,
        features,
        depth_weight,
        depth_slot,
        tile_cells,
    )
    arrived = exchanged(outgoing)

    _, edge = lax.optimization_barrier((outgoing, grad_out))
    gout_edges = jnp.stack(
        [
            edge[:2].reshape(80, CH),
            edge[38:].reshape(80, CH),
            edge[:, :2].reshape(80, CH),
            edge[:, 38:].reshape(80, CH),
        ]
    )
    turned_table = jnp.swapaxes(table, 1, 2)
    _, first_late, second_late = lax.optimization_barrier((outgoing, first_taps, second_taps))
    first_flip, second_flip = flipped(first_late, second_late)
    arrived, turned_table, first_flip, second_flip = lax.optimization_barrier(
        (arrived, turned_table, first_flip, second_flip)
    )

    base, top, bottom, left, right = splat(arrived, gout_edges)
    from_left, from_right = shifted(right, "bx", 1), shifted(left, "bx", -1)
    up, down = with_corners(top, bottom, from_left, from_right)
    rims = (shifted(down, "by", 1), shifted(up, "by", -1), from_left, from_right)
    hidden, fcot, sums = activate_tile(
        spot, first_taps, second_flip, base, grad_out.reshape(CELLS, CH), rims
    )
    arrived, sums = lax.optimization_barrier((arrived, sums))
    codes = arrived[:, 128:130, :64].astype(F32)
    cell_column = (codes[:, 0] * 128 + codes[:, 1]).astype(jnp.int32).reshape(-1, 1)
    pairs = [(i, i ^ 1) for i in range(lax.axis_size("bx"))]
    sums = exchanged(sums.reshape(devices, SHARE, 128))
    returning = send_back(first_flip, cell_column, fcot)
    returned = exchanged(add_share(sums, returning))
    out_bev = outward(second_taps, hidden)
    returned, out_bev = lax.optimization_barrier((returned, out_bev))
    own = returned[:, 128:, :]
    other = lax.ppermute(own, "bx", pairs)
    feature_grad, weight_grad = settle(
        depth_first,
        depth_count,
        patch_count,
        route,
        features,
        depth_weight,
        depth_slot,
        turned_table,
        returned,
    )
    other, weight_grad = lax.optimization_barrier((other, weight_grad))
    grad_first, grad_second = widen(spot, own, other)
    return (
        out_bev.reshape(TILE, TILE, CH),
        feature_grad,
        weight_grad,
        grad_first.reshape(3, 3, CH, CH),
        grad_second.reshape(3, 3, CH, CH),
    )


def solution(mesh):
    placed = (
        P(("by", "bx"), None, None),
        P(("by", "bx"), None, None),
        P(("by", "bx"), None, None),
        P(("by", "bx")),
        P(("by", "bx")),
        P(("by", "bx")),
        P(("by", "bx"), None),
        P(("by", "bx"), None),
        P(),
        P(),
        P("by", "bx", None),
    )
    return jax.shard_map(
        on_device,
        mesh=mesh,
        in_specs=placed,
        out_specs=(
            P("by", "bx", None),
            P(("by", "bx"), None, None),
            P(("by", "bx"), None, None),
            P(),
            P(),
        ),
        check_vma=False,
    )
```
